256 devices in a mesh: pos: 64 (over x, z, core), kvh: 4 (over y).
Axes of the slice: x: 4, y: 4, z: 8, core: 2. Of those that a mesh axis runs over, the one named last changes fastest.
Arguments:
- queries: bfloat16 [256, 64, 128], P('pos', 'kvh'), may hold values from -112 to 112
- prefix_keys: bfloat16 [262144, 8, 128], P('pos', 'kvh'), may hold values from -4 to 4
- prefix_values: bfloat16 [262144, 8, 128], P('pos', 'kvh'), may hold values from -6 to 6
- suffix_keys: bfloat16 [256, 1024, 8, 128], P('pos', None, 'kvh'), may hold values from -6 to 6
- suffix_values: bfloat16 [256, 1024, 8, 128], P('pos', None, 'kvh'), may hold values from -6 to 6
- suffix_lengths: int32 [256], P('pos'), may hold values from 1 to 1024, as said below
Outputs:
- attended: bfloat16 [256, 64, 128], P('pos', 'kvh')
The draws below stay inside these ranges and needn't reach their ends.
Inputs may be any that keep to these rules, and one draw needn't show every extreme that they name: `suffix_lengths`: each request's suffix, its new token included, holds 1 to 1024 tokens; some request holds exactly 1024.
All inputs are finite; a program needn't handle non-finite values.
Results may differ from the reference program's by a relative error of at most 0.008.
Values may be sent and summed in bfloat16 or wider, within the bound.
A program may use at most 64 MiB of HBM per device.

```python
import math
import jax
import jax.numpy as jnp
from jax import lax

HEADS = 64
KVHEADS = 8
HEAD_DIM = 128
SUF = 1024
REQUESTS = 256
PREFIX = 262144


def shared_keys(key):
    base = jnp.clip(jax.random.normal(key, (PREFIX, KVHEADS, HEAD_DIM), jnp.float32), -4.0, 4.0)
    spacing = PREFIX // 8
    position = jnp.arange(PREFIX)
    follows = ((position - 4) % spacing == 0)[:, None, None]
    copied = base
    return jnp.where(follows, copied, base)


def draw_prefix_keys(key, part):
    return shared_keys(key).astype(jnp.bfloat16)


def draw_queries(key, part):
    key = jax.random.fold_in(key, 7)
    first = jax.random.fold_in(key, 0)
    values = jnp.clip(2.5 * jax.random.normal(first, (REQUESTS, HEADS, HEAD_DIM), jnp.float32), -10.0, 10.0)
    return values.astype(jnp.bfloat16)


def draw_suffix_lengths(key, part):
    key = jax.random.fold_in(key, 11)
    first, second = jax.random.split(key)
    lengths = jax.random.randint(first, (REQUESTS,), 1, SUF + 1, jnp.int32)
    chosen = jax.random.randint(second, (), 0, REQUESTS, jnp.int32)
    return jnp.where(jnp.arange(REQUESTS, dtype=jnp.int32) == chosen, SUF, lengths).astype(jnp.int32)


def steps_of(stream_key, dims, shards, least, high):
    loudness, own = 1.0, jax.random.fold_in(stream_key, 6)
    for dim, blocks in shards:
        steps = jnp.exp(jax.random.uniform(jax.random.fold_in(own, dim), (blocks,), jnp.float32, least / len(shards), high / len(shards)))
        loudness = loudness * jnp.repeat(steps, dims[dim] // blocks).reshape([-1 if axis == dim else 1 for axis in range(len(dims))])
    return loudness


def centred(key, shape, width, limit, shards=(), held_as=jnp.bfloat16):
    entries = jax.random.normal(key, shape, jnp.float32) * width
    if len(shards) > 0:
        entries = steps_of(key, shape, shards, -0.22, 0.18) * entries
    return jnp.clip(entries, min=-limit, max=limit).astype(held_as)


def setup_inputs(seed: int = 0) -> dict:
    streams_of = jax.random.split(jax.random.key(seed), 7)
    return {
        "queries": draw_queries(jax.random.fold_in(streams_of[6], 71), 0),
        "prefix_keys": draw_prefix_keys(jax.random.fold_in(streams_of[6], 71), 0),
        "prefix_values": centred(streams_of[2], (PREFIX, KVHEADS, HEAD_DIM), 1.0, 6.0, ((0, 64), (1, 4))),
        "suffix_keys": centred(streams_of[3], (REQUESTS, SUF, KVHEADS, HEAD_DIM), 1.0, 6.0, ((0, 64), (2, 4))),
        "suffix_values": centred(streams_of[4], (REQUESTS, SUF, KVHEADS, HEAD_DIM), 1.0, 6.0, ((0, 64), (2, 4))),
        "suffix_lengths": draw_suffix_lengths(jax.random.fold_in(streams_of[6], 71), 0),
    }


score_scale = 0.08838834764831845


def reference(queries, prefix_keys, prefix_values, suffix_keys, suffix_values, suffix_lengths):
    per_group = HEADS // KVHEADS
    row_block = math.gcd(16, REQUESTS)
    grouped = queries.reshape(REQUESTS, KVHEADS, per_group, HEAD_DIM)

    def one_block(index):
        start = (index * row_block).astype(jnp.int32)
        query_rows = lax.dynamic_slice_in_dim(grouped, start, row_block, 0).astype(jnp.float32)
        suffix_k = lax.dynamic_slice_in_dim(suffix_keys, start, row_block, 0)
        suffix_v = lax.dynamic_slice_in_dim(suffix_values, start, row_block, 0)
        lengths = lax.dynamic_slice_in_dim(suffix_lengths, start, row_block, 0)
        valid = jnp.arange(SUF, dtype=jnp.int32)[None, :] < lengths[:, None]
        results = []
        for group in range(KVHEADS):
            query_group = query_rows[:, group]
            prefix_scores = jnp.einsum('bjd,pd->bjp', query_group, prefix_keys[:, group].astype(jnp.float32)) * score_scale
            suffix_scores = jnp.einsum('bjd,bsd->bjs', query_group, suffix_k[:, :, group].astype(jnp.float32)) * score_scale
            suffix_scores = jnp.where(valid[:, None, :], suffix_scores, -jnp.inf)
            peak = jnp.maximum(prefix_scores.max(-1), suffix_scores.max(-1))
            prefix_weights = jnp.exp(prefix_scores - peak[..., None])
            suffix_weights = jnp.where(valid[:, None, :], jnp.exp(suffix_scores - peak[..., None]), 0.0)
            totals = prefix_weights.sum(-1) + suffix_weights.sum(-1)
            prefix_rounded = prefix_weights.astype(jnp.bfloat16).astype(jnp.float32)
            suffix_rounded = suffix_weights.astype(jnp.bfloat16).astype(jnp.float32)
            summed = jnp.einsum('bjp,pd->bjd', prefix_rounded, prefix_values[:, group].astype(jnp.float32))
            summed = summed + jnp.einsum('bjs,bsd->bjd', suffix_rounded, suffix_v[:, :, group].astype(jnp.float32))
            results.append(summed / totals[..., None])
        return jnp.stack(results, axis=1)

    blocks = lax.map(one_block, jnp.arange(REQUESTS // row_block, dtype=jnp.int32))
    return blocks.reshape(REQUESTS, HEADS, HEAD_DIM).astype(jnp.bfloat16)
```

```python
import functools

import jax
import jax.numpy as jnp
from jax import lax
from jax.experimental import pallas as pl
from jax.experimental.pallas import tpu as pltpu
from jax.sharding import PartitionSpec as P

f32 = jnp.float32
bf16 = jnp.bfloat16
log2e = 1.4426950408889634
scale = 0.08838834764831845 * log2e

X, Z, CORES = 4, 8, 2
REQ, GROUPS, PER, D = 4, 2, 8, 128
ROWS = REQ * PER
KEYS = 4096
SUF = 1024
CHUNKS = 8
LANES = 2 * 4 * ROWS
HALF = LANES // 2
KB = 256
MSG = GROUPS * ROWS + 16
NT = (((1,), (1,)), ((), ()))


def kernel(
    lens, q_ref, k_hbm, v_hbm, sk_hbm, sv_hbm, out_ref,
    kraw, vraw, skraw, svraw, tmp, kg, vt, qall, s_a, s_b, c_a, c_b, res, sib_in, msg_out, msg_in, suf_o, suf_l,
    load_sem, z_send, z_recv, x_send, x_recv, r_send, r_recv, p_send, p_recv, m_send, m_recv,
):
    me = lax.axis_index("pos")
    my_x, my_z, my_core = me // (Z * CORES), (me // CORES) % Z, me % CORES

    def pos_of(dx, dz, dc):
        return (((my_x + dx) % X) * Z + (my_z + dz) % Z) * CORES + (my_core + dc) % CORES

    sibling = {"pos": pos_of(0, 0, 1)}

    loads = [
        pltpu.make_async_copy(src, dst, load_sem.at[n])
        for n, (src, dst) in enumerate(((k_hbm, kraw), (v_hbm, vraw), (sk_hbm, skraw), (sv_hbm, svraw)))
    ]
    for load in loads:
        load.start()

    barrier = pltpu.get_barrier_semaphore()

    def greet(n, carry):
        pl.semaphore_signal(barrier, inc=1, device_id={"pos": pos_of(n // Z, n % Z, 0)}, device_id_type=pl.DeviceIdType.MESH)
        return carry

    lax.fori_loop(1, X * Z, greet, 0)
    pl.semaphore_signal(barrier, inc=1, device_id=sibling, device_id_type=pl.DeviceIdType.MESH)

    mine = q_ref[...].astype(f32).reshape(REQ, GROUPS, PER, D)
    for g in range(GROUPS):
        qall[g, 0, 0, ROWS : 2 * ROWS] = mine[:, g].reshape(ROWS, D).astype(bf16)

    pl.semaphore_wait(barrier, X * Z)

    def z_copy(dz):
        slot = (Z - dz + 1) % Z
        return pltpu.make_async_remote_copy(
            src_ref=qall.at[:, 0, 0, pl.ds(ROWS, ROWS)],
            dst_ref=qall.at[:, 0, slot // 4, pl.ds(pl.multiple_of((slot % 4) * ROWS, ROWS), ROWS)],
            send_sem=z_send.at[dz],
            recv_sem=z_recv.at[Z - dz],
            device_id={"pos": pos_of(0, dz, 0)},
            device_id_type=pl.DeviceIdType.MESH,
        )

    def x_copy(dx):
        return pltpu.make_async_remote_copy(
            src_ref=qall.at[:, 0, :, pl.ds(0, HALF)],
            dst_ref=qall.at[:, X - dx, :, pl.ds(0, HALF)],
            send_sem=x_send.at[dx],
            recv_sem=x_recv.at[X - dx],
            device_id={"pos": pos_of(dx, 0, 0)},
            device_id_type=pl.DeviceIdType.MESH,
        )

    def relay_copy(dx):
        return pltpu.make_async_remote_copy(
            src_ref=qall.at[:, dx, :, pl.ds(0, HALF)],
            dst_ref=qall.at[:, dx, :, pl.ds(HALF, HALF)],
            send_sem=r_send.at[dx],
            recv_sem=r_recv.at[dx],
            device_id=sibling,
            device_id_type=pl.DeviceIdType.MESH,
        )

    def pair_copy(i, g):
        return pltpu.make_async_remote_copy(
            src_ref=res.at[i, g, 1],
            dst_ref=sib_in.at[i, g],
            send_sem=p_send.at[i, g],
            recv_sem=p_recv.at[i, g],
            device_id=sibling,
            device_id_type=pl.DeviceIdType.MESH,
        )

    def msg_copy(dx, dz):
        slot = (dz + 1) % Z
        there = ((X - dx) % X) * Z + (Z - dz) % Z
        return pltpu.make_async_remote_copy(
            src_ref=msg_out.at[dx * Z + slot],
            dst_ref=msg_in.at[there],
            send_sem=m_send.at[dx * Z + dz],
            recv_sem=m_recv.at[there],
            device_id={"pos": pos_of(dx, dz, 0)},
            device_id_type=pl.DeviceIdType.MESH,
        )

    def loop(low, high, do):
        def step(n, carry):
            do(n)
            return carry

        lax.fori_loop(low, high, step, 0)

    loop(1, Z, lambda dz: z_copy(dz).start())

    step = tmp.shape[0]

    def split_keys(n):
        tmp[...] = kraw[pl.ds(pl.multiple_of(n * step, step), step)].astype(f32)
        for g in range(GROUPS):
            kg[g, pl.ds(pl.multiple_of(n * (step // 2), step // 2), step // 2)] = tmp[pl.ds(g, step // 2, stride=2)].astype(bf16)

    def split_values(n):
        tmp[...] = vraw[pl.ds(pl.multiple_of(n * step, step), step)].astype(f32)
        for g in range(GROUPS):
            vt[g, :, pl.ds(pl.multiple_of(n * (step // 2), step // 2), step // 2)] = tmp[pl.ds(g, step // 2, stride=2)].astype(bf16).T

    loads[0].wait()
    loop(0, GROUPS * KEYS // step, split_keys)
    loads[1].wait()
    loop(0, GROUPS * KEYS // step, split_values)

    loop(1, Z, lambda dz: z_copy(Z - dz).wait_recv())
    relay_copy(0).start()
    for dx in (3, 1, 2):
        x_copy(dx).start()

    loads[2].wait()
    loads[3].wait()
    keys = GROUPS * SUF
    row_group = lax.broadcasted_iota(jnp.int32, (GROUPS * PER, keys), 0) // PER
    column = lax.broadcasted_iota(jnp.int32, (GROUPS * PER, keys), 1)
    same_head = row_group == column % GROUPS
    for r in range(REQ):
        rows = pl.ds(r * keys, keys)
        s = lax.dot_general(q_ref[r], skraw[rows], NT, preferred_element_type=f32) * scale
        live = same_head & (column // GROUPS < lens[r])
        s = jnp.where(live, s, -jnp.inf)
        peak = jnp.max(s, axis=1, keepdims=True)
        p = jnp.where(live, jnp.exp2(s - peak), 0.0)
        total = jnp.sum(p, axis=1, keepdims=True)
        o = jnp.dot(p.astype(bf16), svraw[rows], preferred_element_type=f32) / total
        log_total = jnp.broadcast_to(peak + jnp.log(total) * log2e, (GROUPS * PER, D))
        for g in range(GROUPS):
            suf_o[pl.ds(g * ROWS + r * PER, PER)] = o[g * PER : (g + 1) * PER]
            suf_l[pl.ds(g * ROWS + r * PER, PER)] = log_total[g * PER : (g + 1) * PER]

    def phase(qk, pv):
        if qk is not None:
            qv, gq, s_w, c_w = qk
            top = None
        if pv is not None:
            i, gp, s_r, c_r = pv
            c_old = c_r[0:1]
            acc = total = None
        for j in range(KEYS // KB):
            ks = pl.ds(j * KB, KB)
            if qk is not None:
                s = lax.dot_general(kg[gq, ks], qv, NT, preferred_element_type=f32)
                s_w[ks] = s
                m = jnp.max(s.reshape(KB // 8, 8, LANES), axis=0)
                top = m if top is None else jnp.maximum(top, m)
            if pv is not None:
                p = jnp.exp2(s_r[ks] * scale - c_old)
                t = jnp.sum(p.reshape(KB // 8, 8, LANES), axis=0)
                part = jnp.dot(vt[gp, :, ks], p.astype(bf16), preferred_element_type=f32)
                acc = part if acc is None else acc + part
                total = t if total is None else total + t
        if qk is not None:
            c_w[...] = jnp.broadcast_to(jnp.max(top, axis=0, keepdims=True) * scale, c_w.shape)
        if pv is not None:
            sums = jnp.broadcast_to(jnp.sum(total, axis=0, keepdims=True), (8, LANES))
            peaks = jnp.broadcast_to(c_old, (8, LANES))
            for half in range(2):
                lanes = slice(half * HALF, (half + 1) * HALF)
                res[i, gp, half, 0:D] = acc[:, lanes]
                res[i, gp, half, D : D + 8] = peaks[:, lanes]
                res[i, gp, half, D + 8 : D + 16] = sums[:, lanes]
            pair_copy(i, gp).start()

    def queries(g, i):
        return qall[g, i // 2, 1 - i % 2]

    def merge(i):
        dx, half = i // 2, 1 - i % 2
        pieces = []
        for g in range(GROUPS):
            pair_copy(i, g).wait_recv()
            a, b = res.at[i, g, 0], sib_in.at[i, g]
            ca, cb, la, lb = a[D : D + 1], b[D : D + 1], a[D + 8 : D + 9], b[D + 8 : D + 9]
            upper = jnp.maximum(ca, cb)
            wa, wb = jnp.exp2(ca - upper), jnp.exp2(cb - upper)
            total = wa * la + wb * lb
            o = a[0:D] * (wa / total) + b[0:D] * (wb / total)
            rows = o.T.astype(bf16).reshape(4, ROWS, D)
            for n in range(4):
                msg_out[dx * Z + half * 4 + n, g * ROWS : (g + 1) * ROWS] = rows[n]
            log_total = jnp.broadcast_to(upper + jnp.log(total) * log2e, (8, HALF))
            high = log_total.astype(bf16).astype(f32)
            middle = (log_total - high).astype(bf16).astype(f32)
            low = log_total - high - middle
            row = lax.broadcasted_iota(jnp.int32, (8, HALF), 0)
            pieces.append(jnp.where(row == 0, high, jnp.where(row == 1, middle, jnp.where(row == 2, low, 0.0))))
        for n in range(4):
            turned = [p if n == 0 else pltpu.roll(p, HALF - n * ROWS, 1) for p in pieces]
            msg_out[dx * Z + half * 4 + n, GROUPS * ROWS : MSG] = jnp.concatenate(turned, axis=0).astype(bf16)
        for n in range(4):
            if n == 1:

                @pl.when(i == 1)
                def _():
                    msg_in[0] = msg_out[1]

                @pl.when(i != 1)
                def _():
                    msg_copy(dx, (half * 4 + n + Z - 1) % Z).start()
            else:
                msg_copy(dx, (half * 4 + n + Z - 1) % Z).start()

    relay_copy(0).wait_recv()
    phase((queries(0, 0), 0, s_a, c_a), None)

    def chunk(i):
        @pl.when((i % 2 == 1) & (i < CHUNKS - 1))
        def _():
            x_copy(X - (i + 1) // 2).wait_recv()
            relay_copy((i + 1) // 2).start()

        phase((queries(1, i), 1, s_b, c_b), (i, 0, s_a, c_a))

        @pl.when(i > 0)
        def _():
            merge(i - 1)

        @pl.when((i % 2 == 1) & (i < CHUNKS - 1))
        def _():
            relay_copy((i + 1) // 2).wait_recv()

    def full_chunk(i):
        chunk(i)
        phase((queries(0, i + 1), 0, s_a, c_a), (i, 1, s_b, c_b))

    loop(0, CHUNKS - 1, full_chunk)
    last = CHUNKS - 1
    phase((queries(1, last), 1, s_b, c_b), (last, 0, s_a, c_a))
    phase(None, (last, 1, s_b, c_b))
    merge(last - 1)
    merge(last)

    loop(1, Z, lambda dz: z_copy(dz).wait_send())
    loop(1, X, lambda dx: x_copy(dx).wait_send())
    loop(0, X, lambda dx: relay_copy(dx).wait_send())
    for g in range(GROUPS):
        loop(0, CHUNKS, lambda i: pair_copy(i, g).wait_send())
    loop(1, X * Z, lambda n: msg_copy(n // Z, n % Z).wait_send())
    loop(1, X * Z, lambda n: msg_copy(n // Z, n % Z).wait_recv())

    logs = []
    stats = msg_in[:, GROUPS * ROWS : MSG].astype(f32)
    for g in range(GROUPS):
        logs.append(jnp.sum(stats[:, g * 8 : (g + 1) * 8], axis=1).T[0:ROWS])
    logs = jnp.concatenate(logs, axis=0)
    own_log = suf_l[:, 0:1]
    upper = jnp.maximum(jnp.max(logs, axis=1, keepdims=True), own_log)
    weights, own_weight = jnp.exp2(logs - upper), jnp.exp2(own_log - upper)
    total = jnp.sum(weights, axis=1, keepdims=True) + own_weight
    acc = suf_o[...] * own_weight
    for n in range(X * Z):
        acc = acc + weights[:, n : n + 1] * msg_in[n, 0 : GROUPS * ROWS].astype(f32)
    acc = (acc / total).reshape(GROUPS, REQ, PER, D)
    for g in range(GROUPS):
        tmp[pl.ds(g * ROWS, ROWS)] = acc[g].reshape(ROWS, D)
    for r in range(REQ):
        parts = [tmp[pl.ds(g * ROWS + r * PER, PER)] for g in range(GROUPS)]
        out_ref[r] = jnp.concatenate(parts, axis=0).astype(bf16)


def on_device(queries, prefix_keys, prefix_values, suffix_keys, suffix_values, suffix_lengths):
    anywhere = pl.BlockSpec(memory_space=pl.ANY)
    vmem = pl.BlockSpec(memory_space=pltpu.VMEM)
    dma = pltpu.SemaphoreType.DMA
    return pl.pallas_call(
        kernel,
        out_shape=jax.ShapeDtypeStruct(queries.shape, bf16),
        in_specs=[pl.BlockSpec(memory_space=pltpu.SMEM), vmem, anywhere, anywhere, anywhere, anywhere],
        out_specs=vmem,
        scratch_shapes=[
            pltpu.VMEM((GROUPS * KEYS, D), bf16),
            pltpu.VMEM((GROUPS * KEYS, D), bf16),
            pltpu.VMEM((REQ * SUF * GROUPS, D), bf16),
            pltpu.VMEM((REQ * SUF * GROUPS, D), bf16),
            pltpu.VMEM((1024, D), f32),
            pltpu.VMEM((GROUPS, KEYS, D), bf16),
            pltpu.VMEM((GROUPS, D, KEYS), bf16),
            pltpu.VMEM((GROUPS, X, 2, LANES, D), bf16),
            pltpu.VMEM((KEYS, LANES), f32),
            pltpu.VMEM((KEYS, LANES), f32),
            pltpu.VMEM((8, LANES), f32),
            pltpu.VMEM((8, LANES), f32),
            pltpu.VMEM((CHUNKS, GROUPS, 2, D + 16, HALF), f32),
            pltpu.VMEM((CHUNKS, GROUPS, D + 16, HALF), f32),
            pltpu.VMEM((X * Z, MSG, D), bf16),
            pltpu.VMEM((X * Z, MSG, D), bf16),
            pltpu.VMEM((GROUPS * ROWS, D), f32),
            pltpu.VMEM((GROUPS * ROWS, D), f32),
            dma((4,)),
            dma((Z,)), dma((Z,)),
            dma((X,)), dma((X,)),
            dma((X,)), dma((X,)),
            dma((CHUNKS, GROUPS)), dma((CHUNKS, GROUPS)),
            dma((X * Z,)), dma((X * Z,)),
        ],
        compiler_params=pltpu.CompilerParams(collective_id=0, has_side_effects=True, vmem_limit_bytes=56 * 2**20),
        cost_estimate=pl.CostEstimate(flops=9 * 10**9, bytes_accessed=9 * 2**20, transcendentals=17 * 10**6),
    )(
        suffix_lengths,
        queries,
        prefix_keys.reshape(GROUPS * KEYS, D),
        prefix_values.reshape(GROUPS * KEYS, D),
        suffix_keys.reshape(REQ * SUF * GROUPS, D),
        suffix_values.reshape(REQ * SUF * GROUPS, D),
    )


def solution(mesh):
    return jax.shard_map(
        on_device,
        mesh=mesh,
        in_specs=(
            P("pos", "kvh", None),
            P("pos", "kvh", None),
            P("pos", "kvh", None),
            P("pos", None, "kvh", None),
            P("pos", None, "kvh", None),
            P("pos"),
        ),
        out_specs=P("pos", "kvh", None),
        check_vma=False,
    )
```

```python
import functools

import jax
import jax.numpy as jnp
from jax import lax
from jax.experimental import pallas as pl
from jax.experimental.pallas import tpu as pltpu
from jax.sharding import PartitionSpec as P

f32 = jnp.float32
bf16 = jnp.bfloat16
log2e = 1.4426950408889634
scale = 0.08838834764831845 * log2e

X, Z, CORES = 4, 8, 2
REQ, GROUPS, PER, D = 4, 2, 8, 128
ROWS = REQ * PER
KEYS = 4096
SUF = 1024
CHUNKS = 8
ORDER = ((0, 1), (1, 1), (3, 1), (2, 1), (2, 0), (1, 0), (3, 0), (0, 0))
FAR, NEAR = 1, 0
LANES = 2 * 4 * ROWS
HALF = LANES // 2
KB = 256
MSG = GROUPS * ROWS + 16
PART = D + 16
NT = (((1,), (1,)), ((), ()))


def kernel(
    lens, q_ref, k_hbm, v_hbm, sk_hbm, sv_hbm, out_ref,
    kraw, vraw, skraw, svraw, tmp, kg, vt, qall, s_a, s_b, c_a, c_b, res, sib_in, own, x_out, x_in, msg_out, msg_in, suf_o, suf_l,
    load_sem, z_send, z_recv, x_send, x_recv, r_send, r_recv, p_send, p_recv, xm_send, xm_recv, m_send, m_recv,
):
    me = lax.axis_index("pos")
    my_x, my_z, my_core = me // (Z * CORES), (me // CORES) % Z, me % CORES

    def pos_of(dx, dz, dc):
        return (((my_x + dx) % X) * Z + (my_z + dz) % Z) * CORES + (my_core + dc) % CORES

    sibling = {"pos": pos_of(0, 0, 1)}

    loads = [
        pltpu.make_async_copy(src, dst, load_sem.at[n])
        for n, (src, dst) in enumerate(((k_hbm, kraw), (v_hbm, vraw), (sk_hbm, skraw), (sv_hbm, svraw)))
    ]
    for load in loads:
        load.start()

    barrier = pltpu.get_barrier_semaphore()

    def loop(low, high, do):
        def step(n, carry):
            do(n)
            return carry

        lax.fori_loop(low, high, step, 0)

    def greet(device):
        pl.semaphore_signal(barrier, inc=1, device_id=device, device_id_type=pl.DeviceIdType.MESH)

    loop(1, Z, lambda dz: greet({"pos": pos_of(0, dz, 0)}))
    loop(1, X, lambda dx: greet({"pos": pos_of(dx, 0, 0)}))
    greet(sibling)

    mine = q_ref[...].astype(f32).reshape(REQ, GROUPS, PER, D)
    for g in range(GROUPS):
        qall[g, 0, 0, ROWS : 2 * ROWS] = mine[:, g].reshape(ROWS, D).astype(bf16)

    pl.semaphore_wait(barrier, X + Z - 1)

    def z_copy(dz):
        slot = (Z - dz + 1) % Z
        return pltpu.make_async_remote_copy(
            src_ref=qall.at[:, 0, 0, pl.ds(ROWS, ROWS)],
            dst_ref=qall.at[:, 0, slot // 4, pl.ds(pl.multiple_of((slot % 4) * ROWS, ROWS), ROWS)],
            send_sem=z_send.at[dz],
            recv_sem=z_recv.at[Z - dz],
            device_id={"pos": pos_of(0, dz, 0)},
            device_id_type=pl.DeviceIdType.MESH,
        )

    def x_copy(dx, half):
        return pltpu.make_async_remote_copy(
            src_ref=qall.at[:, 0, half, pl.ds(0, HALF)],
            dst_ref=qall.at[:, X - dx, half, pl.ds(0, HALF)],
            send_sem=x_send.at[dx, half],
            recv_sem=x_recv.at[X - dx, half],
            device_id={"pos": pos_of(dx, 0, 0)},
            device_id_type=pl.DeviceIdType.MESH,
        )

    def relay_copy(dx, half):
        return pltpu.make_async_remote_copy(
            src_ref=qall.at[:, dx, half, pl.ds(0, HALF)],
            dst_ref=qall.at[:, dx, half, pl.ds(HALF, HALF)],
            send_sem=r_send.at[dx, half],
            recv_sem=r_recv.at[dx, half],
            device_id=sibling,
            device_id_type=pl.DeviceIdType.MESH,
        )

    def pair_copy(i, g):
        return pltpu.make_async_remote_copy(
            src_ref=res.at[i, g, 1],
            dst_ref=sib_in.at[i, g],
            send_sem=p_send.at[i, g],
            recv_sem=p_recv.at[i, g],
            device_id=sibling,
            device_id_type=pl.DeviceIdType.MESH,
        )

    def part_copy(dx, half, g):
        return pltpu.make_async_remote_copy(
            src_ref=x_out.at[dx, half, g],
            dst_ref=x_in.at[X - dx, half, g],
            send_sem=xm_send.at[dx, half, g],
            recv_sem=xm_recv.at[X - dx, half, g],
            device_id={"pos": pos_of(dx, 0, 0)},
            device_id_type=pl.DeviceIdType.MESH,
        )

    def msg_copy(dz):
        return pltpu.make_async_remote_copy(
            src_ref=msg_out.at[dz],
            dst_ref=msg_in.at[Z - dz],
            send_sem=m_send.at[dz],
            recv_sem=m_recv.at[Z - dz],
            device_id={"pos": pos_of(0, dz, 0)},
            device_id_type=pl.DeviceIdType.MESH,
        )

    loop(1, Z, lambda dz: z_copy(dz).start())

    step = tmp.shape[0]

    def split_keys(n):
        tmp[...] = kraw[pl.ds(pl.multiple_of(n * step, step), step)].astype(f32)
        for g in range(GROUPS):
            kg[g, pl.ds(pl.multiple_of(n * (step // 2), step // 2), step // 2)] = tmp[pl.ds(g, step // 2, stride=2)].astype(bf16)

    def split_values(n):
        tmp[...] = vraw[pl.ds(pl.multiple_of(n * step, step), step)].astype(f32)
        for g in range(GROUPS):
            vt[g, :, pl.ds(pl.multiple_of(n * (step // 2), step // 2), step // 2)] = tmp[pl.ds(g, step // 2, stride=2)].astype(bf16).T

    loads[0].wait()
    loop(0, GROUPS * KEYS // step, split_keys)

    loop(1, Z, lambda dz: z_copy(Z - dz).wait_recv())
    relay_copy(0, FAR).start()
    for dx, half in ((3, FAR), (1, FAR), (2, FAR), (2, NEAR), (3, NEAR), (1, NEAR)):
        x_copy(dx, half).start()
    relay_copy(0, NEAR).start()

    loads[1].wait()
    loop(0, GROUPS * KEYS // step, split_values)

    def suffix(r):
        keys = GROUPS * SUF
        row_group = lax.broadcasted_iota(jnp.int32, (GROUPS * PER, keys), 0) // PER
        column = lax.broadcasted_iota(jnp.int32, (GROUPS * PER, keys), 1)
        live = (row_group == column % GROUPS) & (column // GROUPS < lens[r])
        rows = pl.ds(r * keys, keys)
        s = lax.dot_general(q_ref[r], skraw[rows], NT, preferred_element_type=f32) * scale
        s = jnp.where(live, s, -jnp.inf)
        peak = jnp.max(s, axis=1, keepdims=True)
        p = jnp.where(live, jnp.exp2(s - peak), 0.0)
        total = jnp.sum(p, axis=1, keepdims=True)
        o = jnp.dot(p.astype(bf16), svraw[rows], preferred_element_type=f32) / total
        log_total = jnp.broadcast_to(peak + jnp.log(total) * log2e, (GROUPS * PER, D))
        for g in range(GROUPS):
            suf_o[pl.ds(g * ROWS + r * PER, PER)] = o[g * PER : (g + 1) * PER]
            suf_l[pl.ds(g * ROWS + r * PER, PER)] = log_total[g * PER : (g + 1) * PER]

    def phase(qk, pv):
        if qk is not None:
            qv, gq, s_w, c_w = qk
            top = None
        if pv is not None:
            i, gp, s_r, c_r = pv
            c_old = c_r[0:1]
            acc = total = None
        for j in range(KEYS // KB):
            ks = pl.ds(j * KB, KB)
            if qk is not None:
                s = lax.dot_general(kg[gq, ks], qv, NT, preferred_element_type=f32)
                s_w[ks] = s
                m = jnp.max(s.reshape(KB // 8, 8, LANES), axis=0)
                top = m if top is None else jnp.maximum(top, m)
            if pv is not None:
                p = jnp.exp2(s_r[ks] * scale - c_old)
                t = jnp.sum(p.reshape(KB // 8, 8, LANES), axis=0)
                part = jnp.dot(vt[gp, :, ks], p.astype(bf16), preferred_element_type=f32)
                acc = part if acc is None else acc + part
                total = t if total is None else total + t
        if qk is not None:
            c_w[...] = jnp.broadcast_to(jnp.max(top, axis=0, keepdims=True) * scale, c_w.shape)
        if pv is not None:
            sums = jnp.broadcast_to(jnp.sum(total, axis=0, keepdims=True), (8, LANES))
            peaks = jnp.broadcast_to(c_old, (8, LANES))
            for half in range(2):
                lanes = slice(half * HALF, (half + 1) * HALF)
                res[i, gp, half, 0:D] = acc[:, lanes]
                res[i, gp, half, D : D + 8] = peaks[:, lanes]
                res[i, gp, half, D + 8 : D + 16] = sums[:, lanes]
            pair_copy(i, gp).start()

    def place(i):
        if isinstance(i, int):
            return ORDER[i]
        dx, half = 0, 0
        for n, (a, b) in enumerate(ORDER):
            dx = jnp.where(i == n, a, dx)
            half = jnp.where(i == n, b, half)
        return dx, half

    def queries(g, i):
        dx, half = place(i)
        return qall[g, dx, half]

    def in_three(x):
        high = x.astype(bf16).astype(f32)
        middle = (x - high).astype(bf16).astype(f32)
        row = lax.broadcasted_iota(jnp.int32, x.shape, 0)
        return jnp.where(row == 0, high, jnp.where(row == 1, middle, jnp.where(row == 2, x - high - middle, 0.0)))

    def merge(i, g):
        dx, half = place(i)
        pair_copy(i, g).wait_recv()
        a, b = res.at[i, g, 0], sib_in.at[i, g]
        ca, cb, la, lb = a[D : D + 1], b[D : D + 1], a[D + 8 : D + 9], b[D + 8 : D + 9]
        upper = jnp.maximum(ca, cb)
        wa, wb = jnp.exp2(ca - upper), jnp.exp2(cb - upper)
        total = wa * la + wb * lb
        o = a[0:D] * (wa / total) + b[0:D] * (wb / total)
        log_total = jnp.broadcast_to(upper + jnp.log(total) * log2e, (8, HALF))

        def keep():
            own[half, g, 0:D] = o
            own[half, g, D : D + 8] = log_total

        def send():
            x_out[dx, half, g, 0:D] = o.astype(bf16)
            x_out[dx, half, g, D:PART] = jnp.concatenate([in_three(log_total), jnp.zeros((8, HALF), f32)], axis=0).astype(bf16)
            part_copy(dx, half, g).start()

        if isinstance(i, int):
            keep() if dx == 0 else send()
        else:
            pl.when(i == 0)(keep)
            pl.when(i != 0)(send)

    def merge_x(half):
        pieces = []
        for g in range(GROUPS):
            for dx in range(1, X):
                part_copy(X - dx, half, g).wait_recv()
            logs = [own[half, g, D : D + 1]]
            logs += [jnp.sum(x_in[dx, half, g, D:PART].astype(f32), axis=0, keepdims=True) for dx in range(1, X)]
            upper = functools.reduce(jnp.maximum, logs)
            weights = [jnp.exp2(n - upper) for n in logs]
            total = sum(weights)
            o = own[half, g, 0:D] * (weights[0] / total)
            for dx in range(1, X):
                o = o + x_in[dx, half, g, 0:D].astype(f32) * (weights[dx] / total)
            rows = o.T.astype(bf16)
            for n in range(4):
                msg_out[(half * 4 + n + Z - 1) % Z, g * ROWS : (g + 1) * ROWS] = rows[n * ROWS : (n + 1) * ROWS]
            pieces.append(in_three(jnp.broadcast_to(upper + jnp.log(total) * log2e, (8, HALF))))
        for n in range(4):
            turned = [p if n == 0 else pltpu.roll(p, HALF - n * ROWS, 1) for p in pieces]
            dz = (half * 4 + n + Z - 1) % Z
            msg_out[dz, GROUPS * ROWS : MSG] = jnp.concatenate(turned, axis=0).astype(bf16)
            if dz == 0:
                msg_in[0] = msg_out[0]
            else:
                msg_copy(dz).start()

    relay_copy(0, FAR).wait_recv()
    phase((queries(0, 0), 0, s_a, c_a), None)

    def full_chunk(i):
        dx, half = place(i + 1)

        @pl.when(i < CHUNKS - 2)
        def _():
            x_copy(X - dx, half).wait_recv()
            relay_copy(dx, half).start()

        phase((queries(1, i), 1, s_b, c_b), (i, 0, s_a, c_a))

        @pl.when(i > 0)
        def _():
            merge(i - 1, 0)

        @pl.when(i == CHUNKS - 2)
        def _():
            merge_x(FAR)

        relay_copy(dx, half).wait_recv()
        phase((queries(0, i + 1), 0, s_a, c_a), (i, 1, s_b, c_b))

        @pl.when(i > 0)
        def _():
            merge(i - 1, 1)

    loop(0, CHUNKS - 1, full_chunk)
    last = CHUNKS - 1
    phase((queries(1, last), 1, s_b, c_b), (last, 0, s_a, c_a))
    merge(last - 1, 0)
    merge(last - 1, 1)
    phase(None, (last, 1, s_b, c_b))
    loads[2].wait()
    loads[3].wait()
    suffix(0)
    merge(last, 0)
    suffix(1)
    merge(last, 1)
    merge_x(NEAR)
    suffix(2)
    suffix(3)

    loop(1, Z, lambda dz: z_copy(dz).wait_send())
    for half in range(2):
        loop(1, X, lambda dx: x_copy(dx, half).wait_send())
        loop(0, X, lambda dx: relay_copy(dx, half).wait_send())
        for g in range(GROUPS):
            loop(1, X, lambda dx: part_copy(dx, half, g).wait_send())
    for g in range(GROUPS):
        loop(0, CHUNKS, lambda i: pair_copy(i, g).wait_send())
    loop(1, Z, lambda dz: msg_copy(dz).wait_send())
    loop(1, Z, lambda dz: msg_copy(dz).wait_recv())

    logs = []
    stats = msg_in[:, GROUPS * ROWS : MSG].astype(f32)
    for g in range(GROUPS):
        logs.append(jnp.sum(stats[:, g * 8 : (g + 1) * 8], axis=1).T[0:ROWS])
    logs = jnp.concatenate(logs, axis=0)
    own_log = suf_l[:, 0:1]
    upper = jnp.maximum(jnp.max(logs, axis=1, keepdims=True), own_log)
    weights, own_weight = jnp.exp2(logs - upper), jnp.exp2(own_log - upper)
    total = jnp.sum(weights, axis=1, keepdims=True) + own_weight
    acc = suf_o[...] * own_weight
    for n in range(Z):
        acc = acc + weights[:, n : n + 1] * msg_in[n, 0 : GROUPS * ROWS].astype(f32)
    acc = (acc / total).reshape(GROUPS, REQ, PER, D)
    for g in range(GROUPS):
        tmp[pl.ds(g * ROWS, ROWS)] = acc[g].reshape(ROWS, D)
    for r in range(REQ):
        parts = [tmp[pl.ds(g * ROWS + r * PER, PER)] for g in range(GROUPS)]
        out_ref[r] = jnp.concatenate(parts, axis=0).astype(bf16)


def on_device(queries, prefix_keys, prefix_values, suffix_keys, suffix_values, suffix_lengths):
    anywhere = pl.BlockSpec(memory_space=pl.ANY)
    vmem = pl.BlockSpec(memory_space=pltpu.VMEM)
    dma = pltpu.SemaphoreType.DMA
    return pl.pallas_call(
        kernel,
        out_shape=jax.ShapeDtypeStruct(queries.shape, bf16),
        in_specs=[pl.BlockSpec(memory_space=pltpu.SMEM), vmem, anywhere, anywhere, anywhere, anywhere],
        out_specs=vmem,
        scratch_shapes=[
            pltpu.VMEM((GROUPS * KEYS, D), bf16),
            pltpu.VMEM((GROUPS * KEYS, D), bf16),
            pltpu.VMEM((REQ * SUF * GROUPS, D), bf16),
            pltpu.VMEM((REQ * SUF * GROUPS, D), bf16),
            pltpu.VMEM((1024, D), f32),
            pltpu.VMEM((GROUPS, KEYS, D), bf16),
            pltpu.VMEM((GROUPS, D, KEYS), bf16),
            pltpu.VMEM((GROUPS, X, 2, LANES, D), bf16),
            pltpu.VMEM((KEYS, LANES), f32),
            pltpu.VMEM((KEYS, LANES), f32),
            pltpu.VMEM((8, LANES), f32),
            pltpu.VMEM((8, LANES), f32),
            pltpu.VMEM((CHUNKS, GROUPS, 2, D + 16, HALF), f32),
            pltpu.VMEM((CHUNKS, GROUPS, D + 16, HALF), f32),
            pltpu.VMEM((2, GROUPS, D + 8, HALF), f32),
            pltpu.VMEM((X, 2, GROUPS, PART, HALF), bf16),
            pltpu.VMEM((X, 2, GROUPS, PART, HALF), bf16),
            pltpu.VMEM((Z, MSG, D), bf16),
            pltpu.VMEM((Z, MSG, D), bf16),
            pltpu.VMEM((GROUPS * ROWS, D), f32),
            pltpu.VMEM((GROUPS * ROWS, D), f32),
            dma((4,)),
            dma((Z,)), dma((Z,)),
            dma((X, 2)), dma((X, 2)),
            dma((X, 2)), dma((X, 2)),
            dma((CHUNKS, GROUPS)), dma((CHUNKS, GROUPS)),
            dma((X, 2, GROUPS)), dma((X, 2, GROUPS)),
            dma((Z,)), dma((Z,)),
        ],
        compiler_params=pltpu.CompilerParams(collective_id=0, has_side_effects=True, vmem_limit_bytes=56 * 2**20),
        cost_estimate=pl.CostEstimate(flops=9 * 10**9, bytes_accessed=9 * 2**20, transcendentals=17 * 10**6),
    )(
        suffix_lengths,
        queries,
        prefix_keys.reshape(GROUPS * KEYS, D),
        prefix_values.reshape(GROUPS * KEYS, D),
        suffix_keys.reshape(REQ * SUF * GROUPS, D),
        suffix_values.reshape(REQ * SUF * GROUPS, D),
    )


def solution(mesh):
    return jax.shard_map(
        on_device,
        mesh=mesh,
        in_specs=(
            P("pos", "kvh", None),
            P("pos", "kvh", None),
            P("pos", "kvh", None),
            P("pos", None, "kvh", None),
            P("pos", None, "kvh", None),
            P("pos"),
        ),
        out_specs=P("pos", "kvh", None),
        check_vma=False,
    )
```

```python
import functools

import jax
import jax.numpy as jnp
from jax import lax
from jax.experimental import pallas as pl
from jax.experimental.pallas import tpu as pltpu
from jax.sharding import PartitionSpec as P

f32 = jnp.float32
bf16 = jnp.bfloat16
log2e = 1.4426950408889634
scale = 0.08838834764831845 * log2e

X, Z, CORES = 4, 8, 2
REQ, GROUPS, PER, D = 4, 2, 8, 128
ROWS = REQ * PER
KEYS = 4096
SUF = 1024
CHUNKS = 8
ORDER = ((0, 0), (1, 0), (3, 0), (2, 0), (1, 1), (2, 1), (3, 1), (0, 1))
FAR, NEAR = 1, 0
LANES = 2 * 4 * ROWS
HALF = LANES // 2
KB = 256
MSG = ROWS + 16
PART = D + 16
NT = (((1,), (1,)), ((), ()))


def kernel(
    lens, q_ref, k_hbm, v_hbm, sk_hbm, sv_hbm, out_ref,
    kraw, vraw, skraw, svraw, tmp, kg, vt, qall, s_a, s_b, c_a, c_b, res, sib_in, own, x_out, x_in, msg_out, msg_in, suf_o, suf_l,
    load_sem, z_send, z_recv, x_send, x_recv, r_send, r_recv, p_send, p_recv, xm_send, xm_recv, m_send, m_recv,
):
    me = lax.axis_index("pos")
    my_x, my_z, my_core = me // (Z * CORES), (me // CORES) % Z, me % CORES

    def pos_of(dx, dz, dc):
        return (((my_x + dx) % X) * Z + (my_z + dz) % Z) * CORES + (my_core + dc) % CORES

    sibling = {"pos": pos_of(0, 0, 1)}

    loads = [
        pltpu.make_async_copy(src, dst, load_sem.at[n])
        for n, (src, dst) in enumerate(((k_hbm, kraw), (v_hbm, vraw), (sk_hbm, skraw), (sv_hbm, svraw)))
    ]
    for load in loads:
        load.start()

    barrier = pltpu.get_barrier_semaphore()

    def loop(low, high, do):
        def step(n, carry):
            do(n)
            return carry

        lax.fori_loop(low, high, step, 0)

    def greet(device):
        pl.semaphore_signal(barrier, inc=1, device_id=device, device_id_type=pl.DeviceIdType.MESH)

    loop(1, Z, lambda dz: greet({"pos": pos_of(0, dz, 0)}))
    loop(1, X, lambda dx: greet({"pos": pos_of(dx, 0, 0)}))
    greet(sibling)

    mine = q_ref[...].astype(f32).reshape(REQ, GROUPS, PER, D)
    for g in range(GROUPS):
        qall[g, 0, 0, ROWS : 2 * ROWS] = mine[:, g].reshape(ROWS, D).astype(bf16)

    pl.semaphore_wait(barrier, X + Z - 1)

    def z_copy(dz):
        slot = (Z - dz + 1) % Z
        return pltpu.make_async_remote_copy(
            src_ref=qall.at[:, 0, 0, pl.ds(ROWS, ROWS)],
            dst_ref=qall.at[:, 0, slot // 4, pl.ds(pl.multiple_of((slot % 4) * ROWS, ROWS), ROWS)],
            send_sem=z_send.at[dz],
            recv_sem=z_recv.at[Z - dz],
            device_id={"pos": pos_of(0, dz, 0)},
            device_id_type=pl.DeviceIdType.MESH,
        )

    def x_copy(dx, half):
        return pltpu.make_async_remote_copy(
            src_ref=qall.at[:, 0, half, pl.ds(0, HALF)],
            dst_ref=qall.at[:, X - dx, half, pl.ds(0, HALF)],
            send_sem=x_send.at[dx, half],
            recv_sem=x_recv.at[X - dx, half],
            device_id={"pos": pos_of(dx, 0, 0)},
            device_id_type=pl.DeviceIdType.MESH,
        )

    def relay_copy(dx, half):
        return pltpu.make_async_remote_copy(
            src_ref=qall.at[:, dx, half, pl.ds(0, HALF)],
            dst_ref=qall.at[:, dx, half, pl.ds(HALF, HALF)],
            send_sem=r_send.at[dx, half],
            recv_sem=r_recv.at[dx, half],
            device_id=sibling,
            device_id_type=pl.DeviceIdType.MESH,
        )

    def pair_copy(i, g):
        return pltpu.make_async_remote_copy(
            src_ref=res.at[i, g, 1],
            dst_ref=sib_in.at[i, g],
            send_sem=p_send.at[i, g],
            recv_sem=p_recv.at[i, g],
            device_id=sibling,
            device_id_type=pl.DeviceIdType.MESH,
        )

    def part_copy(dx, half, g):
        return pltpu.make_async_remote_copy(
            src_ref=x_out.at[dx, half, g],
            dst_ref=x_in.at[X - dx, half, g],
            send_sem=xm_send.at[dx, half, g],
            recv_sem=xm_recv.at[X - dx, half, g],
            device_id={"pos": pos_of(dx, 0, 0)},
            device_id_type=pl.DeviceIdType.MESH,
        )

    def msg_copy(dz, g):
        return pltpu.make_async_remote_copy(
            src_ref=msg_out.at[g, dz],
            dst_ref=msg_in.at[g, Z - dz],
            send_sem=m_send.at[g, dz],
            recv_sem=m_recv.at[g, Z - dz],
            device_id={"pos": pos_of(0, dz, 0)},
            device_id_type=pl.DeviceIdType.MESH,
        )

    for dz in (1, 7, 2, 6, 3, 5, 4):
        z_copy(dz).start()

    step = tmp.shape[0]

    def split_keys(n):
        tmp[...] = kraw[pl.ds(pl.multiple_of(n * step, step), step)].astype(f32)
        for g in range(GROUPS):
            kg[g, pl.ds(pl.multiple_of(n * (step // 2), step // 2), step // 2)] = tmp[pl.ds(g, step // 2, stride=2)].astype(bf16)

    def split_values(n):
        tmp[...] = vraw[pl.ds(pl.multiple_of(n * step, step), step)].astype(f32)
        for g in range(GROUPS):
            vt[g, :, pl.ds(pl.multiple_of(n * (step // 2), step // 2), step // 2)] = tmp[pl.ds(g, step // 2, stride=2)].astype(bf16).T

    loads[0].wait()
    loop(0, GROUPS * KEYS // step, split_keys)

    def pass_on(half):
        for dz in (3, 4, 5, 6) if half == FAR else (7, 1, 2):
            z_copy(Z - dz).wait_recv()
        relay_copy(0, half).start()
        for dx in (3, 1, 2):
            x_copy(dx, half).start()

    pass_on(NEAR)
    loads[1].wait()
    loop(0, GROUPS * KEYS // step, split_values)

    def suffix(r):
        keys = GROUPS * SUF
        row_group = lax.broadcasted_iota(jnp.int32, (GROUPS * PER, keys), 0) // PER
        column = lax.broadcasted_iota(jnp.int32, (GROUPS * PER, keys), 1)
        live = (row_group == column % GROUPS) & (column // GROUPS < lens[r])
        rows = pl.ds(r * keys, keys)
        s = lax.dot_general(q_ref[r], skraw[rows], NT, preferred_element_type=f32) * scale
        s = jnp.where(live, s, -jnp.inf)
        peak = jnp.max(s, axis=1, keepdims=True)
        p = jnp.where(live, jnp.exp2(s - peak), 0.0)
        total = jnp.sum(p, axis=1, keepdims=True)
        o = jnp.dot(p.astype(bf16), svraw[rows], preferred_element_type=f32) / total
        log_total = jnp.broadcast_to(peak + jnp.log(total) * log2e, (GROUPS * PER, D))
        for g in range(GROUPS):
            suf_o[pl.ds(g * ROWS + r * PER, PER)] = o[g * PER : (g + 1) * PER]
            suf_l[pl.ds(g * ROWS + r * PER, PER)] = log_total[g * PER : (g + 1) * PER]

    def phase(qk, pv):
        if qk is not None:
            qv, gq, s_w, c_w = qk
            top = None
        if pv is not None:
            i, gp, s_r, c_r = pv
            c_old = c_r[0:1]
            acc = total = None
        for j in range(KEYS // KB):
            ks = pl.ds(j * KB, KB)
            if qk is not None:
                s = lax.dot_general(kg[gq, ks], qv, NT, preferred_element_type=f32)
                s_w[ks] = s
                m = jnp.max(s.reshape(KB // 8, 8, LANES), axis=0)
                top = m if top is None else jnp.maximum(top, m)
            if pv is not None:
                p = jnp.exp2(s_r[ks] * scale - c_old)
                t = jnp.sum(p.reshape(KB // 8, 8, LANES), axis=0)
                part = jnp.dot(vt[gp, :, ks], p.astype(bf16), preferred_element_type=f32)
                acc = part if acc is None else acc + part
                total = t if total is None else total + t
        if qk is not None:
            c_w[...] = jnp.broadcast_to(jnp.max(top, axis=0, keepdims=True) * scale, c_w.shape)
        if pv is not None:
            sums = jnp.broadcast_to(jnp.sum(total, axis=0, keepdims=True), (8, LANES))
            peaks = jnp.broadcast_to(c_old, (8, LANES))
            for half in range(2):
                lanes = slice(half * HALF, (half + 1) * HALF)
                res[i, gp, half, 0:D] = acc[:, lanes]
                res[i, gp, half, D : D + 8] = peaks[:, lanes]
                res[i, gp, half, D + 8 : D + 16] = sums[:, lanes]
            pair_copy(i, gp).start()

    def place(i):
        if isinstance(i, int):
            return ORDER[i]
        dx, half = 0, 0
        for n, (a, b) in enumerate(ORDER):
            dx = jnp.where(i == n, a, dx)
            half = jnp.where(i == n, b, half)
        return dx, half

    def queries(g, i):
        dx, half = place(i)
        return qall[g, dx, half]

    def in_three(x):
        high = x.astype(bf16).astype(f32)
        middle = (x - high).astype(bf16).astype(f32)
        row = lax.broadcasted_iota(jnp.int32, x.shape, 0)
        return jnp.where(row == 0, high, jnp.where(row == 1, middle, jnp.where(row == 2, x - high - middle, 0.0)))

    def merge(i, g):
        dx, half = place(i)
        pair_copy(i, g).wait_recv()
        a, b = res.at[i, g, 0], sib_in.at[i, g]
        ca, cb, la, lb = a[D : D + 1], b[D : D + 1], a[D + 8 : D + 9], b[D + 8 : D + 9]
        upper = jnp.maximum(ca, cb)
        wa, wb = jnp.exp2(ca - upper), jnp.exp2(cb - upper)
        total = wa * la + wb * lb
        o = a[0:D] * (wa / total) + b[0:D] * (wb / total)
        log_total = jnp.broadcast_to(upper + jnp.log(total) * log2e, (8, HALF))

        def keep():
            own[half, g, 0:D] = o
            own[half, g, D : D + 8] = log_total

        def send():
            x_out[dx, half, g, 0:D] = o.astype(bf16)
            x_out[dx, half, g, D:PART] = jnp.concatenate([in_three(log_total), jnp.zeros((8, HALF), f32)], axis=0).astype(bf16)
            part_copy(dx, half, g).start()

        if isinstance(i, int):
            keep() if dx == 0 else send()
        else:
            pl.when(i == 0)(keep)
            pl.when(i != 0)(send)

    def merge_x(half, g):
        for dx in range(1, X):
            part_copy(X - dx, half, g).wait_recv()
        logs = [own[half, g, D : D + 1]]
        logs += [jnp.sum(x_in[dx, half, g, D:PART].astype(f32), axis=0, keepdims=True) for dx in range(1, X)]
        upper = functools.reduce(jnp.maximum, logs)
        weights = [jnp.exp2(n - upper) for n in logs]
        total = sum(weights)
        o = own[half, g, 0:D] * (weights[0] / total)
        for dx in range(1, X):
            o = o + x_in[dx, half, g, 0:D].astype(f32) * (weights[dx] / total)
        rows = o.T.astype(bf16)
        piece = in_three(jnp.broadcast_to(upper + jnp.log(total) * log2e, (8, HALF)))
        for n in (3, 0, 2, 1):
            dz = (half * 4 + n + Z - 1) % Z
            turned = piece if n == 0 else pltpu.roll(piece, HALF - n * ROWS, 1)
            msg_out[g, dz, 0:ROWS] = rows[n * ROWS : (n + 1) * ROWS]
            msg_out[g, dz, ROWS:MSG] = jnp.concatenate([turned, jnp.zeros((8, HALF), f32)], axis=0).astype(bf16)
            if dz == 0:
                msg_in[g, 0] = msg_out[g, 0]
            else:
                msg_copy(dz, g).start()

    def relay(i):
        dx, half = place(i)
        x_copy(X - dx, half).wait_recv()
        relay_copy(dx, half).start()

    relay_copy(0, NEAR).wait_recv()
    phase((queries(0, 0), 0, s_a, c_a), None)
    relay(1)

    def full_chunk(i):
        phase((queries(1, i), 1, s_b, c_b), (i, 0, s_a, c_a))

        @pl.when(i == 0)
        def _():
            pass_on(FAR)

        @pl.when(i > 0)
        def _():
            merge(i - 1, 0)

        @pl.when(i == CHUNKS - 3)
        def _():
            merge_x(NEAR, 0)

        @pl.when(i < CHUNKS - 3)
        def _():
            relay(i + 2)

        dx, half = place(i + 1)
        relay_copy(dx, half).wait_recv()
        phase((queries(0, i + 1), 0, s_a, c_a), (i, 1, s_b, c_b))

        @pl.when(i > 0)
        def _():
            merge(i - 1, 1)

        @pl.when(i == CHUNKS - 3)
        def _():
            merge_x(NEAR, 1)

    loop(0, CHUNKS - 1, full_chunk)
    last = CHUNKS - 1
    phase((queries(1, last), 1, s_b, c_b), (last, 0, s_a, c_a))
    merge(last - 1, 0)
    merge(last - 1, 1)
    phase(None, (last, 1, s_b, c_b))
    loads[2].wait()
    loads[3].wait()
    suffix(0)
    merge(last, 0)
    merge_x(FAR, 0)
    suffix(1)
    merge(last, 1)
    merge_x(FAR, 1)
    suffix(2)
    suffix(3)

    loop(1, Z, lambda dz: z_copy(dz).wait_send())
    for half in range(2):
        loop(1, X, lambda dx: x_copy(dx, half).wait_send())
        loop(0, X, lambda dx: relay_copy(dx, half).wait_send())
        for g in range(GROUPS):
            loop(1, X, lambda dx: part_copy(dx, half, g).wait_send())
    for g in range(GROUPS):
        loop(0, CHUNKS, lambda i: pair_copy(i, g).wait_send())
    for g in range(GROUPS):
        loop(1, Z, lambda dz: msg_copy(dz, g).wait_send())
        loop(1, Z, lambda dz: msg_copy(dz, g).wait_recv())

    logs = []
    for g in range(GROUPS):
        logs.append(jnp.sum(msg_in[g, :, ROWS:MSG].astype(f32), axis=1).T[0:ROWS])
    logs = jnp.concatenate(logs, axis=0)
    own_log = suf_l[:, 0:1]
    upper = jnp.maximum(jnp.max(logs, axis=1, keepdims=True), own_log)
    weights, own_weight = jnp.exp2(logs - upper), jnp.exp2(own_log - upper)
    total = jnp.sum(weights, axis=1, keepdims=True) + own_weight
    acc = suf_o[...] * own_weight
    for n in range(Z):
        acc = acc + weights[:, n : n + 1] * msg_in[:, n, 0:ROWS].astype(f32).reshape(GROUPS * ROWS, D)
    acc = (acc / total).reshape(GROUPS, REQ, PER, D)
    for g in range(GROUPS):
        tmp[pl.ds(g * ROWS, ROWS)] = acc[g].reshape(ROWS, D)
    for r in range(REQ):
        parts = [tmp[pl.ds(g * ROWS + r * PER, PER)] for g in range(GROUPS)]
        out_ref[r] = jnp.concatenate(parts, axis=0).astype(bf16)


def on_device(queries, prefix_keys, prefix_values, suffix_keys, suffix_values, suffix_lengths):
    anywhere = pl.BlockSpec(memory_space=pl.ANY)
    vmem = pl.BlockSpec(memory_space=pltpu.VMEM)
    dma = pltpu.SemaphoreType.DMA
    return pl.pallas_call(
        kernel,
        out_shape=jax.ShapeDtypeStruct(queries.shape, bf16),
        in_specs=[pl.BlockSpec(memory_space=pltpu.SMEM), vmem, anywhere, anywhere, anywhere, anywhere],
        out_specs=vmem,
        scratch_shapes=[
            pltpu.VMEM((GROUPS * KEYS, D), bf16),
            pltpu.VMEM((GROUPS * KEYS, D), bf16),
            pltpu.VMEM((REQ * SUF * GROUPS, D), bf16),
            pltpu.VMEM((REQ * SUF * GROUPS, D), bf16),
            pltpu.VMEM((1024, D), f32),
            pltpu.VMEM((GROUPS, KEYS, D), bf16),
            pltpu.VMEM((GROUPS, D, KEYS), bf16),
            pltpu.VMEM((GROUPS, X, 2, LANES, D), bf16),
            pltpu.VMEM((KEYS, LANES), f32),
            pltpu.VMEM((KEYS, LANES), f32),
            pltpu.VMEM((8, LANES), f32),
            pltpu.VMEM((8, LANES), f32),
            pltpu.VMEM((CHUNKS, GROUPS, 2, D + 16, HALF), f32),
            pltpu.VMEM((CHUNKS, GROUPS, D + 16, HALF), f32),
            pltpu.VMEM((2, GROUPS, D + 8, HALF), f32),
            pltpu.VMEM((X, 2, GROUPS, PART, HALF), bf16),
            pltpu.VMEM((X, 2, GROUPS, PART, HALF), bf16),
            pltpu.VMEM((GROUPS, Z, MSG, D), bf16),
            pltpu.VMEM((GROUPS, Z, MSG, D), bf16),
            pltpu.VMEM((GROUPS * ROWS, D), f32),
            pltpu.VMEM((GROUPS * ROWS, D), f32),
            dma((4,)),
            dma((Z,)), dma((Z,)),
            dma((X, 2)), dma((X, 2)),
            dma((X, 2)), dma((X, 2)),
            dma((CHUNKS, GROUPS)), dma((CHUNKS, GROUPS)),
            dma((X, 2, GROUPS)), dma((X, 2, GROUPS)),
            dma((GROUPS, Z)), dma((GROUPS, Z)),
        ],
        compiler_params=pltpu.CompilerParams(collective_id=0, has_side_effects=True, vmem_limit_bytes=56 * 2**20),
        cost_estimate=pl.CostEstimate(flops=9 * 10**9, bytes_accessed=9 * 2**20, transcendentals=17 * 10**6),
    )(
        suffix_lengths,
        queries,
        prefix_keys.reshape(GROUPS * KEYS, D),
        prefix_values.reshape(GROUPS * KEYS, D),
        suffix_keys.reshape(REQ * SUF * GROUPS, D),
        suffix_values.reshape(REQ * SUF * GROUPS, D),
    )


def solution(mesh):
    return jax.shard_map(
        on_device,
        mesh=mesh,
        in_specs=(
            P("pos", "kvh", None),
            P("pos", "kvh", None),
            P("pos", "kvh", None),
            P("pos", None, "kvh", None),
            P("pos", None, "kvh", None),
            P("pos"),
        ),
        out_specs=P("pos", "kvh", None),
        check_vma=False,
    )
```

```python
import functools

import jax
import jax.numpy as jnp
from jax import lax
from jax.experimental import pallas as pl
from jax.experimental.pallas import tpu as pltpu
from jax.sharding import PartitionSpec as P

f32 = jnp.float32
bf16 = jnp.bfloat16
log2e = 1.4426950408889634
scale = 0.08838834764831845 * log2e

X, Z, CORES = 4, 8, 2
REQ, GROUPS, PER, D = 4, 2, 8, 128
ROWS = REQ * PER
KEYS = 4096
SUF = 1024
CHUNKS = 8
ORDER = ((0, 0), (1, 0), (3, 0), (2, 0), (1, 1), (2, 1), (3, 1), (0, 1))
FAR, NEAR = 1, 0
SIDE = (0, 7, 1, 6)
LANES = 2 * 4 * ROWS
HALF = LANES // 2
KB = 256
MSG = ROWS + 16
PART = D + 16
NT = (((1,), (1,)), ((), ()))


def kernel(
    lens, q_ref, k_hbm, v_hbm, sk_hbm, sv_hbm, out_ref,
    kraw, vraw, skraw, svraw, tmp, kg, vt, qall, s_a, s_b, c_a, c_b, res, sib_in, own, x_out, x_in, msg_out, msg_in, suf_o, suf_l,
    load_sem, z_send, z_recv, d_send, d_recv, x_send, x_recv, r_send, r_recv, p_send, p_recv, xm_send, xm_recv, m_send, m_recv,
):
    me = lax.axis_index("pos")
    my_x, my_z, my_core = me // (Z * CORES), (me // CORES) % Z, me % CORES

    def pos_of(dx, dz, dc):
        return (((my_x + dx) % X) * Z + (my_z + dz) % Z) * CORES + (my_core + dc) % CORES

    sibling = {"pos": pos_of(0, 0, 1)}

    loads = [
        pltpu.make_async_copy(src, dst, load_sem.at[n])
        for n, (src, dst) in enumerate(((k_hbm, kraw), (v_hbm, vraw), (sk_hbm, skraw), (sv_hbm, svraw)))
    ]
    for load in loads:
        load.start()

    barrier = pltpu.get_barrier_semaphore()

    def loop(low, high, do):
        def step(n, carry):
            do(n)
            return carry

        lax.fori_loop(low, high, step, 0)

    def greet(device):
        pl.semaphore_signal(barrier, inc=1, device_id=device, device_id_type=pl.DeviceIdType.MESH)

    loop(1, Z, lambda dz: greet({"pos": pos_of(0, dz, 0)}))
    loop(1, X, lambda dx: greet({"pos": pos_of(dx, 0, 0)}))
    greet(sibling)
    for dz in SIDE[1:]:
        greet({"pos": pos_of(1, Z - dz, 0)})

    mine = q_ref[...].astype(f32).reshape(REQ, GROUPS, PER, D)
    for g in range(GROUPS):
        qall[g, 0, 0, ROWS : 2 * ROWS] = mine[:, g].reshape(ROWS, D).astype(bf16)

    pl.semaphore_wait(barrier, X + Z - 1 + len(SIDE) - 1)

    def z_copy(dz):
        slot = (Z - dz + 1) % Z
        return pltpu.make_async_remote_copy(
            src_ref=qall.at[:, 0, 0, pl.ds(ROWS, ROWS)],
            dst_ref=qall.at[:, 0, slot // 4, pl.ds(pl.multiple_of((slot % 4) * ROWS, ROWS), ROWS)],
            send_sem=z_send.at[dz],
            recv_sem=z_recv.at[Z - dz],
            device_id={"pos": pos_of(0, dz, 0)},
            device_id_type=pl.DeviceIdType.MESH,
        )

    def side_copy(dz):
        slot = (Z - dz + 1) % Z
        return pltpu.make_async_remote_copy(
            src_ref=qall.at[:, 0, NEAR, pl.ds(ROWS, ROWS)],
            dst_ref=qall.at[:, 1, NEAR, pl.ds(slot * ROWS, ROWS)],
            send_sem=d_send.at[slot],
            recv_sem=d_recv.at[slot],
            device_id={"pos": pos_of(X - 1, dz, 0)},
            device_id_type=pl.DeviceIdType.MESH,
        )

    def x_copy(dx, half):
        return pltpu.make_async_remote_copy(
            src_ref=qall.at[:, 0, half, pl.ds(0, HALF)],
            dst_ref=qall.at[:, X - dx, half, pl.ds(0, HALF)],
            send_sem=x_send.at[dx, half],
            recv_sem=x_recv.at[X - dx, half],
            device_id={"pos": pos_of(dx, 0, 0)},
            device_id_type=pl.DeviceIdType.MESH,
        )

    def relay_copy(dx, half):
        return pltpu.make_async_remote_copy(
            src_ref=qall.at[:, dx, half, pl.ds(0, HALF)],
            dst_ref=qall.at[:, dx, half, pl.ds(HALF, HALF)],
            send_sem=r_send.at[dx, half],
            recv_sem=r_recv.at[dx, half],
            device_id=sibling,
            device_id_type=pl.DeviceIdType.MESH,
        )

    def pair_copy(i, g):
        return pltpu.make_async_remote_copy(
            src_ref=res.at[i, g, 1],
            dst_ref=sib_in.at[i, g],
            send_sem=p_send.at[i, g],
            recv_sem=p_recv.at[i, g],
            device_id=sibling,
            device_id_type=pl.DeviceIdType.MESH,
        )

    def part_copy(dx, half, g):
        return pltpu.make_async_remote_copy(
            src_ref=x_out.at[dx, half, g],
            dst_ref=x_in.at[X - dx, half, g],
            send_sem=xm_send.at[dx, half, g],
            recv_sem=xm_recv.at[X - dx, half, g],
            device_id={"pos": pos_of(dx, 0, 0)},
            device_id_type=pl.DeviceIdType.MESH,
        )

    def msg_copy(dz, g):
        return pltpu.make_async_remote_copy(
            src_ref=msg_out.at[g, dz],
            dst_ref=msg_in.at[g, Z - dz],
            send_sem=m_send.at[g, dz],
            recv_sem=m_recv.at[g, Z - dz],
            device_id={"pos": pos_of(0, dz, 0)},
            device_id_type=pl.DeviceIdType.MESH,
        )

    for dz in (1, 7, 2):
        z_copy(dz).start()
    for dz in SIDE:
        side_copy(dz).start()
    for dz in (6, 3, 5, 4):
        z_copy(dz).start()

    step = tmp.shape[0]

    def split_keys(n):
        tmp[...] = kraw[pl.ds(pl.multiple_of(n * step, step), step)].astype(f32)
        for g in range(GROUPS):
            kg[g, pl.ds(pl.multiple_of(n * (step // 2), step // 2), step // 2)] = tmp[pl.ds(g, step // 2, stride=2)].astype(bf16)

    def split_values(n):
        tmp[...] = vraw[pl.ds(pl.multiple_of(n * step, step), step)].astype(f32)
        for g in range(GROUPS):
            vt[g, :, pl.ds(pl.multiple_of(n * (step // 2), step // 2), step // 2)] = tmp[pl.ds(g, step // 2, stride=2)].astype(bf16).T

    loads[0].wait()
    loop(0, GROUPS * KEYS // step, split_keys)
    loads[1].wait()
    loop(0, GROUPS * KEYS // step, split_values)

    def pass_on(half):
        for dz in (3, 4, 5, 6) if half == FAR else (7, 1, 2):
            z_copy(Z - dz).wait_recv()
        relay_copy(0, half).start()
        for dx in (3, 1, 2) if half == FAR else (1, 2):
            x_copy(dx, half).start()

    pass_on(NEAR)

    def suffix(r):
        keys = GROUPS * SUF
        row_group = lax.broadcasted_iota(jnp.int32, (GROUPS * PER, keys), 0) // PER
        column = lax.broadcasted_iota(jnp.int32, (GROUPS * PER, keys), 1)
        live = (row_group == column % GROUPS) & (column // GROUPS < lens[r])
        rows = pl.ds(r * keys, keys)
        s = lax.dot_general(q_ref[r], skraw[rows], NT, preferred_element_type=f32) * scale
        s = jnp.where(live, s, -jnp.inf)
        peak = jnp.max(s, axis=1, keepdims=True)
        p = jnp.where(live, jnp.exp2(s - peak), 0.0)
        total = jnp.sum(p, axis=1, keepdims=True)
        o = jnp.dot(p.astype(bf16), svraw[rows], preferred_element_type=f32) / total
        log_total = jnp.broadcast_to(peak + jnp.log(total) * log2e, (GROUPS * PER, D))
        for g in range(GROUPS):
            suf_o[pl.ds(g * ROWS + r * PER, PER)] = o[g * PER : (g + 1) * PER]
            suf_l[pl.ds(g * ROWS + r * PER, PER)] = log_total[g * PER : (g + 1) * PER]

    def phase(qk, pv):
        if qk is not None:
            qv, gq, s_w, c_w = qk
            top = None
        if pv is not None:
            i, gp, s_r, c_r = pv
            c_old = c_r[0:1]
            acc = total = None
        for j in range(KEYS // KB):
            ks = pl.ds(j * KB, KB)
            if qk is not None:
                s = lax.dot_general(kg[gq, ks], qv, NT, preferred_element_type=f32)
                s_w[ks] = s
                m = jnp.max(s.reshape(KB // 8, 8, LANES), axis=0)
                top = m if top is None else jnp.maximum(top, m)
            if pv is not None:
                p = jnp.exp2(s_r[ks] * scale - c_old)
                t = jnp.sum(p.reshape(KB // 8, 8, LANES), axis=0)
                part = jnp.dot(vt[gp, :, ks], p.astype(bf16), preferred_element_type=f32)
                acc = part if acc is None else acc + part
                total = t if total is None else total + t
        if qk is not None:
            c_w[...] = jnp.broadcast_to(jnp.max(top, axis=0, keepdims=True) * scale, c_w.shape)
        if pv is not None:
            sums = jnp.broadcast_to(jnp.sum(total, axis=0, keepdims=True), (8, LANES))
            peaks = jnp.broadcast_to(c_old, (8, LANES))
            for half in range(2):
                lanes = slice(half * HALF, (half + 1) * HALF)
                res[i, gp, half, 0:D] = acc[:, lanes]
                res[i, gp, half, D : D + 8] = peaks[:, lanes]
                res[i, gp, half, D + 8 : D + 16] = sums[:, lanes]
            pair_copy(i, gp).start()

    def place(i):
        if isinstance(i, int):
            return ORDER[i]
        dx, half = 0, 0
        for n, (a, b) in enumerate(ORDER):
            dx = jnp.where(i == n, a, dx)
            half = jnp.where(i == n, b, half)
        return dx, half

    def queries(g, i):
        dx, half = place(i)
        return qall[g, dx, half]

    def in_three(x):
        high = x.astype(bf16).astype(f32)
        middle = (x - high).astype(bf16).astype(f32)
        row = lax.broadcasted_iota(jnp.int32, x.shape, 0)
        return jnp.where(row == 0, high, jnp.where(row == 1, middle, jnp.where(row == 2, x - high - middle, 0.0)))

    def merge(i, g):
        dx, half = place(i)
        pair_copy(i, g).wait_recv()
        a, b = res.at[i, g, 0], sib_in.at[i, g]
        ca, cb, la, lb = a[D : D + 1], b[D : D + 1], a[D + 8 : D + 9], b[D + 8 : D + 9]
        upper = jnp.maximum(ca, cb)
        wa, wb = jnp.exp2(ca - upper), jnp.exp2(cb - upper)
        total = wa * la + wb * lb
        o = a[0:D] * (wa / total) + b[0:D] * (wb / total)
        log_total = jnp.broadcast_to(upper + jnp.log(total) * log2e, (8, HALF))

        def keep():
            own[half, g, 0:D] = o
            own[half, g, D : D + 8] = log_total

        def send():
            x_out[dx, half, g, 0:D] = o.astype(bf16)
            x_out[dx, half, g, D:PART] = jnp.concatenate([in_three(log_total), jnp.zeros((8, HALF), f32)], axis=0).astype(bf16)
            part_copy(dx, half, g).start()

        if isinstance(i, int):
            keep() if dx == 0 else send()
        else:
            pl.when(i == 0)(keep)
            pl.when(i != 0)(send)

    def merge_x(half, g):
        for dx in range(1, X):
            part_copy(X - dx, half, g).wait_recv()
        logs = [own[half, g, D : D + 1]]
        logs += [jnp.sum(x_in[dx, half, g, D:PART].astype(f32), axis=0, keepdims=True) for dx in range(1, X)]
        upper = functools.reduce(jnp.maximum, logs)
        weights = [jnp.exp2(n - upper) for n in logs]
        total = sum(weights)
        o = own[half, g, 0:D] * (weights[0] / total)
        for dx in range(1, X):
            o = o + x_in[dx, half, g, 0:D].astype(f32) * (weights[dx] / total)
        rows = o.T.astype(bf16)
        piece = in_three(jnp.broadcast_to(upper + jnp.log(total) * log2e, (8, HALF)))
        for n in (3, 0, 2, 1):
            dz = (half * 4 + n + Z - 1) % Z
            turned = piece if n == 0 else pltpu.roll(piece, HALF - n * ROWS, 1)
            msg_out[g, dz, 0:ROWS] = rows[n * ROWS : (n + 1) * ROWS]
            msg_out[g, dz, ROWS:MSG] = jnp.concatenate([turned, jnp.zeros((8, HALF), f32)], axis=0).astype(bf16)
            if dz == 0:
                msg_in[g, 0] = msg_out[g, 0]
            else:
                msg_copy(dz, g).start()

    def relay(i):
        dx, half = place(i)
        x_copy(X - dx, half).wait_recv()
        relay_copy(dx, half).start()

    relay_copy(0, NEAR).wait_recv()
    phase((queries(0, 0), 0, s_a, c_a), None)
    for dz in SIDE:
        side_copy(dz).wait_recv()
    relay_copy(1, NEAR).start()

    def full_chunk(i):
        phase((queries(1, i), 1, s_b, c_b), (i, 0, s_a, c_a))

        @pl.when(i > 0)
        def _():
            merge(i - 1, 0)

        @pl.when(i == CHUNKS - 3)
        def _():
            merge_x(NEAR, 0)

        @pl.when(i < CHUNKS - 3)
        def _():
            relay(i + 2)

        dx, half = place(i + 1)
        relay_copy(dx, half).wait_recv()
        phase((queries(0, i + 1), 0, s_a, c_a), (i, 1, s_b, c_b))

        @pl.when(i == 0)
        def _():
            pass_on(FAR)

        @pl.when(i > 0)
        def _():
            merge(i - 1, 1)

        @pl.when(i == CHUNKS - 3)
        def _():
            merge_x(NEAR, 1)

    loop(0, CHUNKS - 1, full_chunk)
    last = CHUNKS - 1
    merge(last - 1, 0)
    phase((queries(1, last), 1, s_b, c_b), (last, 0, s_a, c_a))
    merge(last - 1, 1)
    phase(None, (last, 1, s_b, c_b))
    loads[2].wait()
    loads[3].wait()
    suffix(0)
    merge(last, 0)
    suffix(1)
    merge(last, 1)
    merge_x(FAR, 0)
    suffix(2)
    merge_x(FAR, 1)
    suffix(3)

    for dz in SIDE:
        side_copy(dz).wait_send()
    loop(1, Z, lambda dz: z_copy(dz).wait_send())
    for half in range(2):
        loop(1, X if half == FAR else X - 1, lambda dx: x_copy(dx, half).wait_send())
        loop(0, X, lambda dx: relay_copy(dx, half).wait_send())
        for g in range(GROUPS):
            loop(1, X, lambda dx: part_copy(dx, half, g).wait_send())
    for g in range(GROUPS):
        loop(0, CHUNKS, lambda i: pair_copy(i, g).wait_send())
    for g in range(GROUPS):
        loop(1, Z, lambda dz: msg_copy(dz, g).wait_send())
        loop(1, Z, lambda dz: msg_copy(dz, g).wait_recv())

    logs = []
    for g in range(GROUPS):
        logs.append(jnp.sum(msg_in[g, :, ROWS:MSG].astype(f32), axis=1).T[0:ROWS])
    logs = jnp.concatenate(logs, axis=0)
    own_log = suf_l[:, 0:1]
    upper = jnp.maximum(jnp.max(logs, axis=1, keepdims=True), own_log)
    weights, own_weight = jnp.exp2(logs - upper), jnp.exp2(own_log - upper)
    total = jnp.sum(weights, axis=1, keepdims=True) + own_weight
    acc = suf_o[...] * own_weight
    for n in range(Z):
        acc = acc + weights[:, n : n + 1] * msg_in[:, n, 0:ROWS].astype(f32).reshape(GROUPS * ROWS, D)
    acc = (acc / total).reshape(GROUPS, REQ, PER, D)
    for g in range(GROUPS):
        tmp[pl.ds(g * ROWS, ROWS)] = acc[g].reshape(ROWS, D)
    for r in range(REQ):
        parts = [tmp[pl.ds(g * ROWS + r * PER, PER)] for g in range(GROUPS)]
        out_ref[r] = jnp.concatenate(parts, axis=0).astype(bf16)


def on_device(queries, prefix_keys, prefix_values, suffix_keys, suffix_values, suffix_lengths):
    anywhere = pl.BlockSpec(memory_space=pl.ANY)
    vmem = pl.BlockSpec(memory_space=pltpu.VMEM)
    dma = pltpu.SemaphoreType.DMA
    return pl.pallas_call(
        kernel,
        out_shape=jax.ShapeDtypeStruct(queries.shape, bf16),
        in_specs=[pl.BlockSpec(memory_space=pltpu.SMEM), vmem, anywhere, anywhere, anywhere, anywhere],
        out_specs=vmem,
        scratch_shapes=[
            pltpu.VMEM((GROUPS * KEYS, D), bf16),
            pltpu.VMEM((GROUPS * KEYS, D), bf16),
            pltpu.VMEM((REQ * SUF * GROUPS, D), bf16),
            pltpu.VMEM((REQ * SUF * GROUPS, D), bf16),
            pltpu.VMEM((1024, D), f32),
            pltpu.VMEM((GROUPS, KEYS, D), bf16),
            pltpu.VMEM((GROUPS, D, KEYS), bf16),
            pltpu.VMEM((GROUPS, X, 2, LANES, D), bf16),
            pltpu.VMEM((KEYS, LANES), f32),
            pltpu.VMEM((KEYS, LANES), f32),
            pltpu.VMEM((8, LANES), f32),
            pltpu.VMEM((8, LANES), f32),
            pltpu.VMEM((CHUNKS, GROUPS, 2, D + 16, HALF), f32),
            pltpu.VMEM((CHUNKS, GROUPS, D + 16, HALF), f32),
            pltpu.VMEM((2, GROUPS, D + 8, HALF), f32),
            pltpu.VMEM((X, 2, GROUPS, PART, HALF), bf16),
            pltpu.VMEM((X, 2, GROUPS, PART, HALF), bf16),
            pltpu.VMEM((GROUPS, Z, MSG, D), bf16),
            pltpu.VMEM((GROUPS, Z, MSG, D), bf16),
            pltpu.VMEM((GROUPS * ROWS, D), f32),
            pltpu.VMEM((GROUPS * ROWS, D), f32),
            dma((4,)),
            dma((Z,)), dma((Z,)),
            dma((4,)), dma((4,)),
            dma((X, 2)), dma((X, 2)),
            dma((X, 2)), dma((X, 2)),
            dma((CHUNKS, GROUPS)), dma((CHUNKS, GROUPS)),
            dma((X, 2, GROUPS)), dma((X, 2, GROUPS)),
            dma((GROUPS, Z)), dma((GROUPS, Z)),
        ],
        compiler_params=pltpu.CompilerParams(collective_id=0, has_side_effects=True, vmem_limit_bytes=56 * 2**20),
        cost_estimate=pl.CostEstimate(flops=9 * 10**9, bytes_accessed=9 * 2**20, transcendentals=17 * 10**6),
    )(
        suffix_lengths,
        queries,
        prefix_keys.reshape(GROUPS * KEYS, D),
        prefix_values.reshape(GROUPS * KEYS, D),
        suffix_keys.reshape(REQ * SUF * GROUPS, D),
        suffix_values.reshape(REQ * SUF * GROUPS, D),
    )


def solution(mesh):
    return jax.shard_map(
        on_device,
        mesh=mesh,
        in_specs=(
            P("pos", "kvh", None),
            P("pos", "kvh", None),
            P("pos", "kvh", None),
            P("pos", None, "kvh", None),
            P("pos", None, "kvh", None),
            P("pos"),
        ),
        out_specs=P("pos", "kvh", None),
        check_vma=False,
    )
```

```python
import functools

import jax
import jax.numpy as jnp
from jax import lax
from jax.experimental import pallas as pl
from jax.experimental.pallas import tpu as pltpu
from jax.sharding import PartitionSpec as P

f32 = jnp.float32
bf16 = jnp.bfloat16
log2e = 1.4426950408889634
scale = 0.08838834764831845 * log2e

X, Z, CORES = 4, 8, 2
REQ, GROUPS, PER, D = 4, 2, 8, 128
ROWS = REQ * PER
KEYS = 4096
SUF = 1024
CHUNKS = 8
ORDER = ((0, 1), (1, 1), (3, 1), (2, 1), (2, 0), (1, 0), (3, 0), (0, 0))
FAR, NEAR = 1, 0
LANES = 2 * 4 * ROWS
HALF = LANES // 2
KB = 256
MSG = GROUPS * ROWS + 16
PART = D + 16
NT = (((1,), (1,)), ((), ()))


def kernel(
    lens, q_ref, k_hbm, v_hbm, sk_hbm, sv_hbm, out_ref,
    kraw, vraw, skraw, svraw, tmp, kg, vt, qall, s_a, s_b, c_a, c_b, res, sib_in, own, x_out, x_in, msg_out, msg_in, suf_o, suf_l,
    load_sem, z_send, z_recv, x_send, x_recv, r_send, r_recv, p_send, p_recv, xm_send, xm_recv, m_send, m_recv,
):
    me = lax.axis_index("pos")
    my_x, my_z, my_core = me // (Z * CORES), (me // CORES) % Z, me % CORES

    def pos_of(dx, dz, dc):
        return (((my_x + dx) % X) * Z + (my_z + dz) % Z) * CORES + (my_core + dc) % CORES

    sibling = {"pos": pos_of(0, 0, 1)}

    loads = [
        pltpu.make_async_copy(src, dst, load_sem.at[n])
        for n, (src, dst) in enumerate(((k_hbm, kraw), (v_hbm, vraw), (sk_hbm, skraw), (sv_hbm, svraw)))
    ]
    for load in loads:
        load.start()

    barrier = pltpu.get_barrier_semaphore()

    def loop(low, high, do):
        def step(n, carry):
            do(n)
            return carry

        lax.fori_loop(low, high, step, 0)

    def greet(device):
        pl.semaphore_signal(barrier, inc=1, device_id=device, device_id_type=pl.DeviceIdType.MESH)

    loop(1, Z, lambda dz: greet({"pos": pos_of(0, dz, 0)}))
    loop(1, X, lambda dx: greet({"pos": pos_of(dx, 0, 0)}))
    greet(sibling)

    mine = q_ref[...].astype(f32).reshape(REQ, GROUPS, PER, D)
    for g in range(GROUPS):
        qall[g, 0, 0, ROWS : 2 * ROWS] = mine[:, g].reshape(ROWS, D).astype(bf16)

    pl.semaphore_wait(barrier, X + Z - 1)

    def z_copy(dz):
        slot = (Z - dz + 1) % Z
        return pltpu.make_async_remote_copy(
            src_ref=qall.at[:, 0, 0, pl.ds(ROWS, ROWS)],
            dst_ref=qall.at[:, 0, slot // 4, pl.ds(pl.multiple_of((slot % 4) * ROWS, ROWS), ROWS)],
            send_sem=z_send.at[dz],
            recv_sem=z_recv.at[Z - dz],
            device_id={"pos": pos_of(0, dz, 0)},
            device_id_type=pl.DeviceIdType.MESH,
        )

    def x_copy(dx, half):
        return pltpu.make_async_remote_copy(
            src_ref=qall.at[:, 0, half, pl.ds(0, HALF)],
            dst_ref=qall.at[:, X - dx, half, pl.ds(0, HALF)],
            send_sem=x_send.at[dx, half],
            recv_sem=x_recv.at[X - dx, half],
            device_id={"pos": pos_of(dx, 0, 0)},
            device_id_type=pl.DeviceIdType.MESH,
        )

    def relay_copy(dx, half):
        return pltpu.make_async_remote_copy(
            src_ref=qall.at[:, dx, half, pl.ds(0, HALF)],
            dst_ref=qall.at[:, dx, half, pl.ds(HALF, HALF)],
            send_sem=r_send.at[dx, half],
            recv_sem=r_recv.at[dx, half],
            device_id=sibling,
            device_id_type=pl.DeviceIdType.MESH,
        )

    def pair_copy(i, g):
        return pltpu.make_async_remote_copy(
            src_ref=res.at[i, g, 1],
            dst_ref=sib_in.at[i, g],
            send_sem=p_send.at[i, g],
            recv_sem=p_recv.at[i, g],
            device_id=sibling,
            device_id_type=pl.DeviceIdType.MESH,
        )

    def part_copy(dx, half, g):
        return pltpu.make_async_remote_copy(
            src_ref=x_out.at[dx, half, g],
            dst_ref=x_in.at[X - dx, half, g],
            send_sem=xm_send.at[dx, half, g],
            recv_sem=xm_recv.at[X - dx, half, g],
            device_id={"pos": pos_of(dx, 0, 0)},
            device_id_type=pl.DeviceIdType.MESH,
        )

    def msg_copy(dz):
        return pltpu.make_async_remote_copy(
            src_ref=msg_out.at[dz],
            dst_ref=msg_in.at[Z - dz],
            send_sem=m_send.at[dz],
            recv_sem=m_recv.at[Z - dz],
            device_id={"pos": pos_of(0, dz, 0)},
            device_id_type=pl.DeviceIdType.MESH,
        )

    for dz in (4, 3, 5, 6, 2, 1, 7):
        z_copy(dz).start()

    step = tmp.shape[0]

    def split_keys(n):
        tmp[...] = kraw[pl.ds(pl.multiple_of(n * step, step), step)].astype(f32)
        for g in range(GROUPS):
            kg[g, pl.ds(pl.multiple_of(n * (step // 2), step // 2), step // 2)] = tmp[pl.ds(g, step // 2, stride=2)].astype(bf16)

    def split_values(n):
        tmp[...] = vraw[pl.ds(pl.multiple_of(n * step, step), step)].astype(f32)
        for g in range(GROUPS):
            vt[g, :, pl.ds(pl.multiple_of(n * (step // 2), step // 2), step // 2)] = tmp[pl.ds(g, step // 2, stride=2)].astype(bf16).T

    loads[0].wait()
    loop(0, GROUPS * KEYS // step, split_keys)

    for dz in (3, 4, 5, 6):
        z_copy(Z - dz).wait_recv()
    relay_copy(0, FAR).start()
    for dx in (3, 1, 2):
        x_copy(dx, FAR).start()
    for dz in (7, 1, 2):
        z_copy(Z - dz).wait_recv()
    for dx in (2, 3, 1):
        x_copy(dx, NEAR).start()
    relay_copy(0, NEAR).start()

    loads[1].wait()
    loop(0, GROUPS * KEYS // step, split_values)

    def suffix(r):
        keys = GROUPS * SUF
        row_group = lax.broadcasted_iota(jnp.int32, (GROUPS * PER, keys), 0) // PER
        column = lax.broadcasted_iota(jnp.int32, (GROUPS * PER, keys), 1)
        live = (row_group == column % GROUPS) & (column // GROUPS < lens[r])
        rows = pl.ds(r * keys, keys)
        s = lax.dot_general(q_ref[r], skraw[rows], NT, preferred_element_type=f32) * scale
        s = jnp.where(live, s, -jnp.inf)
        peak = jnp.max(s, axis=1, keepdims=True)
        p = jnp.where(live, jnp.exp2(s - peak), 0.0)
        total = jnp.sum(p, axis=1, keepdims=True)
        o = jnp.dot(p.astype(bf16), svraw[rows], preferred_element_type=f32) / total
        log_total = jnp.broadcast_to(peak + jnp.log(total) * log2e, (GROUPS * PER, D))
        for g in range(GROUPS):
            suf_o[pl.ds(g * ROWS + r * PER, PER)] = o[g * PER : (g + 1) * PER]
            suf_l[pl.ds(g * ROWS + r * PER, PER)] = log_total[g * PER : (g + 1) * PER]

    def phase(qk, pv):
        if qk is not None:
            qv, gq, s_w, c_w = qk
            top = None
        if pv is not None:
            i, gp, s_r, c_r = pv
            c_old = c_r[0:1]
            acc = total = None
        for j in range(KEYS // KB):
            ks = pl.ds(j * KB, KB)
            if qk is not None:
                s = lax.dot_general(kg[gq, ks], qv, NT, preferred_element_type=f32)
                s_w[ks] = s
                m = jnp.max(s.reshape(KB // 8, 8, LANES), axis=0)
                top = m if top is None else jnp.maximum(top, m)
            if pv is not None:
                p = jnp.exp2(s_r[ks] * scale - c_old)
                t = jnp.sum(p.reshape(KB // 8, 8, LANES), axis=0)
                part = jnp.dot(vt[gp, :, ks], p.astype(bf16), preferred_element_type=f32)
                acc = part if acc is None else acc + part
                total = t if total is None else total + t
        if qk is not None:
            c_w[...] = jnp.broadcast_to(jnp.max(top, axis=0, keepdims=True) * scale, c_w.shape)
        if pv is not None:
            sums = jnp.broadcast_to(jnp.sum(total, axis=0, keepdims=True), (8, LANES))
            peaks = jnp.broadcast_to(c_old, (8, LANES))
            for half in range(2):
                lanes = slice(half * HALF, (half + 1) * HALF)
                res[i, gp, half, 0:D] = acc[:, lanes]
                res[i, gp, half, D : D + 8] = peaks[:, lanes]
                res[i, gp, half, D + 8 : D + 16] = sums[:, lanes]
            pair_copy(i, gp).start()

    def place(i):
        if isinstance(i, int):
            return ORDER[i]
        dx, half = 0, 0
        for n, (a, b) in enumerate(ORDER):
            dx = jnp.where(i == n, a, dx)
            half = jnp.where(i == n, b, half)
        return dx, half

    def queries(g, i):
        dx, half = place(i)
        return qall[g, dx, half]

    def in_three(x):
        high = x.astype(bf16).astype(f32)
        middle = (x - high).astype(bf16).astype(f32)
        row = lax.broadcasted_iota(jnp.int32, x.shape, 0)
        return jnp.where(row == 0, high, jnp.where(row == 1, middle, jnp.where(row == 2, x - high - middle, 0.0)))

    def merge(i, g):
        dx, half = place(i)
        pair_copy(i, g).wait_recv()
        a, b = res.at[i, g, 0], sib_in.at[i, g]
        ca, cb, la, lb = a[D : D + 1], b[D : D + 1], a[D + 8 : D + 9], b[D + 8 : D + 9]
        upper = jnp.maximum(ca, cb)
        wa, wb = jnp.exp2(ca - upper), jnp.exp2(cb - upper)
        total = wa * la + wb * lb
        o = a[0:D] * (wa / total) + b[0:D] * (wb / total)
        log_total = jnp.broadcast_to(upper + jnp.log(total) * log2e, (8, HALF))

        def keep():
            own[half, g, 0:D] = o
            own[half, g, D : D + 8] = log_total

        def send():
            x_out[dx, half, g, 0:D] = o.astype(bf16)
            x_out[dx, half, g, D:PART] = jnp.concatenate([in_three(log_total), jnp.zeros((8, HALF), f32)], axis=0).astype(bf16)
            part_copy(dx, half, g).start()

        if isinstance(i, int):
            keep() if dx == 0 else send()
        else:
            pl.when(i == 0)(keep)
            pl.when(i != 0)(send)

    def merge_x(half):
        pieces = []
        for g in range(GROUPS):
            for dx in range(1, X):
                part_copy(X - dx, half, g).wait_recv()
            logs = [own[half, g, D : D + 1]]
            logs += [jnp.sum(x_in[dx, half, g, D:PART].astype(f32), axis=0, keepdims=True) for dx in range(1, X)]
            upper = functools.reduce(jnp.maximum, logs)
            weights = [jnp.exp2(n - upper) for n in logs]
            total = sum(weights)
            o = own[half, g, 0:D] * (weights[0] / total)
            for dx in range(1, X):
                o = o + x_in[dx, half, g, 0:D].astype(f32) * (weights[dx] / total)
            rows = o.T.astype(bf16)
            for n in range(4):
                msg_out[(half * 4 + n + Z - 1) % Z, g * ROWS : (g + 1) * ROWS] = rows[n * ROWS : (n + 1) * ROWS]
            pieces.append(in_three(jnp.broadcast_to(upper + jnp.log(total) * log2e, (8, HALF))))
        for n in range(4):
            turned = [p if n == 0 else pltpu.roll(p, HALF - n * ROWS, 1) for p in pieces]
            dz = (half * 4 + n + Z - 1) % Z
            msg_out[dz, GROUPS * ROWS : MSG] = jnp.concatenate(turned, axis=0).astype(bf16)
            if dz == 0:
                msg_in[0] = msg_out[0]
            else:
                msg_copy(dz).start()

    relay_copy(0, FAR).wait_recv()
    phase((queries(0, 0), 0, s_a, c_a), None)

    def full_chunk(i):
        dx, half = place(i + 1)

        @pl.when(i < CHUNKS - 2)
        def _():
            x_copy(X - dx, half).wait_recv()
            relay_copy(dx, half).start()

        phase((queries(1, i), 1, s_b, c_b), (i, 0, s_a, c_a))

        @pl.when(i > 0)
        def _():
            merge(i - 1, 0)

        @pl.when(i == CHUNKS - 2)
        def _():
            merge_x(FAR)

        relay_copy(dx, half).wait_recv()
        phase((queries(0, i + 1), 0, s_a, c_a), (i, 1, s_b, c_b))

        @pl.when(i > 0)
        def _():
            merge(i - 1, 1)

    loop(0, CHUNKS - 1, full_chunk)
    last = CHUNKS - 1
    phase((queries(1, last), 1, s_b, c_b), (last, 0, s_a, c_a))
    merge(last - 1, 0)
    merge(last - 1, 1)
    phase(None, (last, 1, s_b, c_b))
    merge(last, 0)
    merge(last, 1)
    merge_x(NEAR)
    loads[2].wait()
    loads[3].wait()
    suffix(0)
    suffix(1)
    suffix(2)
    suffix(3)

    loop(1, Z, lambda dz: z_copy(dz).wait_send())
    for half in range(2):
        loop(1, X, lambda dx: x_copy(dx, half).wait_send())
        loop(0, X, lambda dx: relay_copy(dx, half).wait_send())
        for g in range(GROUPS):
            loop(1, X, lambda dx: part_copy(dx, half, g).wait_send())
    for g in range(GROUPS):
        loop(0, CHUNKS, lambda i: pair_copy(i, g).wait_send())
    loop(1, Z, lambda dz: msg_copy(dz).wait_send())
    loop(1, Z, lambda dz: msg_copy(dz).wait_recv())

    logs = []
    stats = msg_in[:, GROUPS * ROWS : MSG].astype(f32)
    for g in range(GROUPS):
        logs.append(jnp.sum(stats[:, g * 8 : (g + 1) * 8], axis=1).T[0:ROWS])
    logs = jnp.concatenate(logs, axis=0)
    own_log = suf_l[:, 0:1]
    upper = jnp.maximum(jnp.max(logs, axis=1, keepdims=True), own_log)
    weights, own_weight = jnp.exp2(logs - upper), jnp.exp2(own_log - upper)
    total = jnp.sum(weights, axis=1, keepdims=True) + own_weight
    acc = suf_o[...] * own_weight
    for n in range(Z):
        acc = acc + weights[:, n : n + 1] * msg_in[n, 0 : GROUPS * ROWS].astype(f32)
    acc = (acc / total).reshape(GROUPS, REQ, PER, D)
    for g in range(GROUPS):
        tmp[pl.ds(g * ROWS, ROWS)] = acc[g].reshape(ROWS, D)
    for r in range(REQ):
        parts = [tmp[pl.ds(g * ROWS + r * PER, PER)] for g in range(GROUPS)]
        out_ref[r] = jnp.concatenate(parts, axis=0).astype(bf16)


def on_device(queries, prefix_keys, prefix_values, suffix_keys, suffix_values, suffix_lengths):
    anywhere = pl.BlockSpec(memory_space=pl.ANY)
    vmem = pl.BlockSpec(memory_space=pltpu.VMEM)
    dma = pltpu.SemaphoreType.DMA
    return pl.pallas_call(
        kernel,
        out_shape=jax.ShapeDtypeStruct(queries.shape, bf16),
        in_specs=[pl.BlockSpec(memory_space=pltpu.SMEM), vmem, anywhere, anywhere, anywhere, anywhere],
        out_specs=vmem,
        scratch_shapes=[
            pltpu.VMEM((GROUPS * KEYS, D), bf16),
            pltpu.VMEM((GROUPS * KEYS, D), bf16),
            pltpu.VMEM((REQ * SUF * GROUPS, D), bf16),
            pltpu.VMEM((REQ * SUF * GROUPS, D), bf16),
            pltpu.VMEM((1024, D), f32),
            pltpu.VMEM((GROUPS, KEYS, D), bf16),
            pltpu.VMEM((GROUPS, D, KEYS), bf16),
            pltpu.VMEM((GROUPS, X, 2, LANES, D), bf16),
            pltpu.VMEM((KEYS, LANES), f32),
            pltpu.VMEM((KEYS, LANES), f32),
            pltpu.VMEM((8, LANES), f32),
            pltpu.VMEM((8, LANES), f32),
            pltpu.VMEM((CHUNKS, GROUPS, 2, D + 16, HALF), f32),
            pltpu.VMEM((CHUNKS, GROUPS, D + 16, HALF), f32),
            pltpu.VMEM((2, GROUPS, D + 8, HALF), f32),
            pltpu.VMEM((X, 2, GROUPS, PART, HALF), bf16),
            pltpu.VMEM((X, 2, GROUPS, PART, HALF), bf16),
            pltpu.VMEM((Z, MSG, D), bf16),
            pltpu.VMEM((Z, MSG, D), bf16),
            pltpu.VMEM((GROUPS * ROWS, D), f32),
            pltpu.VMEM((GROUPS * ROWS, D), f32),
            dma((4,)),
            dma((Z,)), dma((Z,)),
            dma((X, 2)), dma((X, 2)),
            dma((X, 2)), dma((X, 2)),
            dma((CHUNKS, GROUPS)), dma((CHUNKS, GROUPS)),
            dma((X, 2, GROUPS)), dma((X, 2, GROUPS)),
            dma((Z,)), dma((Z,)),
        ],
        compiler_params=pltpu.CompilerParams(collective_id=0, has_side_effects=True, vmem_limit_bytes=56 * 2**20),
        cost_estimate=pl.CostEstimate(flops=9 * 10**9, bytes_accessed=9 * 2**20, transcendentals=17 * 10**6),
    )(
        suffix_lengths,
        queries,
        prefix_keys.reshape(GROUPS * KEYS, D),
        prefix_values.reshape(GROUPS * KEYS, D),
        suffix_keys.reshape(REQ * SUF * GROUPS, D),
        suffix_values.reshape(REQ * SUF * GROUPS, D),
    )


def solution(mesh):
    return jax.shard_map(
        on_device,
        mesh=mesh,
        in_specs=(
            P("pos", "kvh", None),
            P("pos", "kvh", None),
            P("pos", "kvh", None),
            P("pos", None, "kvh", None),
            P("pos", None, "kvh", None),
            P("pos"),
        ),
        out_specs=P("pos", "kvh", None),
        check_vma=False,
    )
```

```python
import functools

import jax
import jax.numpy as jnp
from jax import lax
from jax.experimental import pallas as pl
from jax.experimental.pallas import tpu as pltpu
from jax.sharding import PartitionSpec as P

f32 = jnp.float32
bf16 = jnp.bfloat16
log2e = 1.4426950408889634
scale = 0.08838834764831845 * log2e

X, Z, CORES = 4, 8, 2
REQ, GROUPS, PER, D = 4, 2, 8, 128
ROWS = REQ * PER
KEYS = 4096
SUF = 1024
CHUNKS = 8
ORDER = ((0, 1), (1, 1), (3, 1), (2, 1), (2, 0), (1, 0), (3, 0), (0, 0))
FAR, NEAR = 1, 0
LANES = 2 * 4 * ROWS
HALF = LANES // 2
KB = 256
MSG = GROUPS * ROWS + 16
PART = D + 16
NT = (((1,), (1,)), ((), ()))


def kernel(
    lens, q_ref, k_hbm, v_hbm, sk_hbm, sv_hbm, out_ref,
    kraw, vraw, skraw, svraw, tmp, kg, vt, qall, s_a, s_b, c_a, c_b, res, sib_in, own, x_out, x_in, msg_out, msg_in, suf_o, suf_l,
    load_sem, z_send, z_recv, x_send, x_recv, r_send, r_recv, p_send, p_recv, xm_send, xm_recv, m_send, m_recv,
):
    me = lax.axis_index("pos")
    my_x, my_z, my_core = me // (Z * CORES), (me // CORES) % Z, me % CORES

    def pos_of(dx, dz, dc):
        return (((my_x + dx) % X) * Z + (my_z + dz) % Z) * CORES + (my_core + dc) % CORES

    sibling = {"pos": pos_of(0, 0, 1)}

    loads = [
        pltpu.make_async_copy(src, dst, load_sem.at[n])
        for n, (src, dst) in enumerate(((k_hbm, kraw), (v_hbm, vraw), (sk_hbm, skraw), (sv_hbm, svraw)))
    ]
    for load in loads:
        load.start()

    barrier = pltpu.get_barrier_semaphore()

    def loop(low, high, do):
        def step(n, carry):
            do(n)
            return carry

        lax.fori_loop(low, high, step, 0)

    def greet(device):
        pl.semaphore_signal(barrier, inc=1, device_id=device, device_id_type=pl.DeviceIdType.MESH)

    loop(1, Z, lambda dz: greet({"pos": pos_of(0, dz, 0)}))
    loop(1, X, lambda dx: greet({"pos": pos_of(dx, 0, 0)}))
    greet(sibling)

    mine = q_ref[...].astype(f32).reshape(REQ, GROUPS, PER, D)
    for g in range(GROUPS):
        qall[g, 0, 0, ROWS : 2 * ROWS] = mine[:, g].reshape(ROWS, D).astype(bf16)

    pl.semaphore_wait(barrier, X + Z - 1)

    def z_copy(dz):
        slot = (Z - dz + 1) % Z
        return pltpu.make_async_remote_copy(
            src_ref=qall.at[:, 0, 0, pl.ds(ROWS, ROWS)],
            dst_ref=qall.at[:, 0, slot // 4, pl.ds(pl.multiple_of((slot % 4) * ROWS, ROWS), ROWS)],
            send_sem=z_send.at[dz],
            recv_sem=z_recv.at[Z - dz],
            device_id={"pos": pos_of(0, dz, 0)},
            device_id_type=pl.DeviceIdType.MESH,
        )

    def x_copy(dx, half):
        return pltpu.make_async_remote_copy(
            src_ref=qall.at[:, 0, half, pl.ds(0, HALF)],
            dst_ref=qall.at[:, X - dx, half, pl.ds(0, HALF)],
            send_sem=x_send.at[dx, half],
            recv_sem=x_recv.at[X - dx, half],
            device_id={"pos": pos_of(dx, 0, 0)},
            device_id_type=pl.DeviceIdType.MESH,
        )

    def relay_copy(dx, half):
        return pltpu.make_async_remote_copy(
            src_ref=qall.at[:, dx, half, pl.ds(0, HALF)],
            dst_ref=qall.at[:, dx, half, pl.ds(HALF, HALF)],
            send_sem=r_send.at[dx, half],
            recv_sem=r_recv.at[dx, half],
            device_id=sibling,
            device_id_type=pl.DeviceIdType.MESH,
        )

    def pair_copy(i, g):
        return pltpu.make_async_remote_copy(
            src_ref=res.at[i, g, 1],
            dst_ref=sib_in.at[i, g],
            send_sem=p_send.at[i, g],
            recv_sem=p_recv.at[i, g],
            device_id=sibling,
            device_id_type=pl.DeviceIdType.MESH,
        )

    def part_copy(dx, half, g):
        return pltpu.make_async_remote_copy(
            src_ref=x_out.at[dx, half, g],
            dst_ref=x_in.at[X - dx, half, g],
            send_sem=xm_send.at[dx, half, g],
            recv_sem=xm_recv.at[X - dx, half, g],
            device_id={"pos": pos_of(dx, 0, 0)},
            device_id_type=pl.DeviceIdType.MESH,
        )

    def msg_copy(dz):
        return pltpu.make_async_remote_copy(
            src_ref=msg_out.at[dz],
            dst_ref=msg_in.at[Z - dz],
            send_sem=m_send.at[dz],
            recv_sem=m_recv.at[Z - dz],
            device_id={"pos": pos_of(0, dz, 0)},
            device_id_type=pl.DeviceIdType.MESH,
        )

    for dz in (4, 3, 5, 6, 2, 1, 7):
        z_copy(dz).start()

    step = tmp.shape[0]

    def split_keys(n):
        tmp[...] = kraw[pl.ds(pl.multiple_of(n * step, step), step)].astype(f32)
        for g in range(GROUPS):
            kg[g, pl.ds(pl.multiple_of(n * (step // 2), step // 2), step // 2)] = tmp[pl.ds(g, step // 2, stride=2)].astype(bf16)

    def split_values(n):
        tmp[...] = vraw[pl.ds(pl.multiple_of(n * step, step), step)].astype(f32)
        for g in range(GROUPS):
            vt[g, :, pl.ds(pl.multiple_of(n * (step // 2), step // 2), step // 2)] = tmp[pl.ds(g, step // 2, stride=2)].astype(bf16).T

    loads[0].wait()
    loop(0, GROUPS * KEYS // step, split_keys)

    for dz in (3, 4, 5, 6):
        z_copy(Z - dz).wait_recv()
    relay_copy(0, FAR).start()
    for dx in (3, 1, 2):
        x_copy(dx, FAR).start()
    def pass_on_near():
        for dz in (7, 1, 2):
            z_copy(Z - dz).wait_recv()
        for dx in (2, 3, 1):
            x_copy(dx, NEAR).start()
        relay_copy(0, NEAR).start()


    loads[1].wait()
    loop(0, GROUPS * KEYS // step, split_values)

    def suffix(r):
        keys = GROUPS * SUF
        row_group = lax.broadcasted_iota(jnp.int32, (GROUPS * PER, keys), 0) // PER
        column = lax.broadcasted_iota(jnp.int32, (GROUPS * PER, keys), 1)
        live = (row_group == column % GROUPS) & (column // GROUPS < lens[r])
        rows = pl.ds(r * keys, keys)
        s = lax.dot_general(q_ref[r], skraw[rows], NT, preferred_element_type=f32) * scale
        s = jnp.where(live, s, -jnp.inf)
        peak = jnp.max(s, axis=1, keepdims=True)
        p = jnp.where(live, jnp.exp2(s - peak), 0.0)
        total = jnp.sum(p, axis=1, keepdims=True)
        o = jnp.dot(p.astype(bf16), svraw[rows], preferred_element_type=f32) / total
        log_total = jnp.broadcast_to(peak + jnp.log(total) * log2e, (GROUPS * PER, D))
        for g in range(GROUPS):
            suf_o[pl.ds(g * ROWS + r * PER, PER)] = o[g * PER : (g + 1) * PER]
            suf_l[pl.ds(g * ROWS + r * PER, PER)] = log_total[g * PER : (g + 1) * PER]

    def phase(qk, pv):
        if qk is not None:
            qv, gq, s_w, c_w = qk
            top = None
        if pv is not None:
            i, gp, s_r, c_r = pv
            c_old = c_r[0:1]
            acc = total = None
        for j in range(KEYS // KB):
            ks = pl.ds(j * KB, KB)
            if qk is not None:
                s = lax.dot_general(kg[gq, ks], qv, NT, preferred_element_type=f32)
                s_w[ks] = s
                m = jnp.max(s.reshape(KB // 8, 8, LANES), axis=0)
                top = m if top is None else jnp.maximum(top, m)
            if pv is not None:
                p = jnp.exp2(s_r[ks] * scale - c_old)
                t = jnp.sum(p.reshape(KB // 8, 8, LANES), axis=0)
                part = jnp.dot(vt[gp, :, ks], p.astype(bf16), preferred_element_type=f32)
                acc = part if acc is None else acc + part
                total = t if total is None else total + t
        if qk is not None:
            c_w[...] = jnp.broadcast_to(jnp.max(top, axis=0, keepdims=True) * scale, c_w.shape)
        if pv is not None:
            sums = jnp.broadcast_to(jnp.sum(total, axis=0, keepdims=True), (8, LANES))
            peaks = jnp.broadcast_to(c_old, (8, LANES))
            for half in range(2):
                lanes = slice(half * HALF, (half + 1) * HALF)
                res[i, gp, half, 0:D] = acc[:, lanes]
                res[i, gp, half, D : D + 8] = peaks[:, lanes]
                res[i, gp, half, D + 8 : D + 16] = sums[:, lanes]
            pair_copy(i, gp).start()

    def place(i):
        if isinstance(i, int):
            return ORDER[i]
        dx, half = 0, 0
        for n, (a, b) in enumerate(ORDER):
            dx = jnp.where(i == n, a, dx)
            half = jnp.where(i == n, b, half)
        return dx, half

    def queries(g, i):
        dx, half = place(i)
        return qall[g, dx, half]

    def in_three(x):
        high = x.astype(bf16).astype(f32)
        middle = (x - high).astype(bf16).astype(f32)
        row = lax.broadcasted_iota(jnp.int32, x.shape, 0)
        return jnp.where(row == 0, high, jnp.where(row == 1, middle, jnp.where(row == 2, x - high - middle, 0.0)))

    def merge(i, g):
        dx, half = place(i)
        pair_copy(i, g).wait_recv()
        a, b = res.at[i, g, 0], sib_in.at[i, g]
        ca, cb, la, lb = a[D : D + 1], b[D : D + 1], a[D + 8 : D + 9], b[D + 8 : D + 9]
        upper = jnp.maximum(ca, cb)
        wa, wb = jnp.exp2(ca - upper), jnp.exp2(cb - upper)
        total = wa * la + wb * lb
        o = a[0:D] * (wa / total) + b[0:D] * (wb / total)
        log_total = jnp.broadcast_to(upper + jnp.log(total) * log2e, (8, HALF))

        def keep():
            own[half, g, 0:D] = o
            own[half, g, D : D + 8] = log_total

        def send():
            x_out[dx, half, g, 0:D] = o.astype(bf16)
            x_out[dx, half, g, D:PART] = jnp.concatenate([in_three(log_total), jnp.zeros((8, HALF), f32)], axis=0).astype(bf16)
            part_copy(dx, half, g).start()

        if isinstance(i, int):
            keep() if dx == 0 else send()
        else:
            pl.when(i == 0)(keep)
            pl.when(i != 0)(send)

    def merge_x(half):
        pieces = []
        for g in range(GROUPS):
            for dx in range(1, X):
                part_copy(X - dx, half, g).wait_recv()
            logs = [own[half, g, D : D + 1]]
            logs += [jnp.sum(x_in[dx, half, g, D:PART].astype(f32), axis=0, keepdims=True) for dx in range(1, X)]
            upper = functools.reduce(jnp.maximum, logs)
            weights = [jnp.exp2(n - upper) for n in logs]
            total = sum(weights)
            o = own[half, g, 0:D] * (weights[0] / total)
            for dx in range(1, X):
                o = o + x_in[dx, half, g, 0:D].astype(f32) * (weights[dx] / total)
            rows = o.T.astype(bf16)
            for n in range(4):
                msg_out[(half * 4 + n + Z - 1) % Z, g * ROWS : (g + 1) * ROWS] = rows[n * ROWS : (n + 1) * ROWS]
            pieces.append(in_three(jnp.broadcast_to(upper + jnp.log(total) * log2e, (8, HALF))))
        for n in range(4):
            turned = [p if n == 0 else pltpu.roll(p, HALF - n * ROWS, 1) for p in pieces]
            dz = (half * 4 + n + Z - 1) % Z
            msg_out[dz, GROUPS * ROWS : MSG] = jnp.concatenate(turned, axis=0).astype(bf16)
            if dz == 0:
                msg_in[0] = msg_out[0]
            else:
                msg_copy(dz).start()

    relay_copy(0, FAR).wait_recv()
    phase((queries(0, 0), 0, s_a, c_a), None)

    def full_chunk(i):
        dx, half = place(i + 1)

        @pl.when(i < CHUNKS - 2)
        def _():
            x_copy(X - dx, half).wait_recv()
            relay_copy(dx, half).start()

        phase((queries(1, i), 1, s_b, c_b), (i, 0, s_a, c_a))

        @pl.when(i > 0)
        def _():
            merge(i - 1, 0)

        @pl.when(i == CHUNKS - 2)
        def _():
            merge_x(FAR)

        pl.when(i == 0)(pass_on_near)
        relay_copy(dx, half).wait_recv()
        phase((queries(0, i + 1), 0, s_a, c_a), (i, 1, s_b, c_b))

        @pl.when(i > 0)
        def _():
            merge(i - 1, 1)

    loop(0, CHUNKS - 1, full_chunk)
    last = CHUNKS - 1
    phase((queries(1, last), 1, s_b, c_b), (last, 0, s_a, c_a))
    merge(last - 1, 0)
    merge(last - 1, 1)
    phase(None, (last, 1, s_b, c_b))
    merge(last, 0)
    merge(last, 1)
    merge_x(NEAR)
    loads[2].wait()
    loads[3].wait()
    suffix(0)
    suffix(1)
    suffix(2)
    suffix(3)

    loop(1, Z, lambda dz: z_copy(dz).wait_send())
    for half in range(2):
        loop(1, X, lambda dx: x_copy(dx, half).wait_send())
        loop(0, X, lambda dx: relay_copy(dx, half).wait_send())
        for g in range(GROUPS):
            loop(1, X, lambda dx: part_copy(dx, half, g).wait_send())
    for g in range(GROUPS):
        loop(0, CHUNKS, lambda i: pair_copy(i, g).wait_send())
    loop(1, Z, lambda dz: msg_copy(dz).wait_send())
    loop(1, Z, lambda dz: msg_copy(dz).wait_recv())

    logs = []
    stats = msg_in[:, GROUPS * ROWS : MSG].astype(f32)
    for g in range(GROUPS):
        logs.append(jnp.sum(stats[:, g * 8 : (g + 1) * 8], axis=1).T[0:ROWS])
    logs = jnp.concatenate(logs, axis=0)
    own_log = suf_l[:, 0:1]
    upper = jnp.maximum(jnp.max(logs, axis=1, keepdims=True), own_log)
    weights, own_weight = jnp.exp2(logs - upper), jnp.exp2(own_log - upper)
    total = jnp.sum(weights, axis=1, keepdims=True) + own_weight
    acc = suf_o[...] * own_weight
    for n in range(Z):
        acc = acc + weights[:, n : n + 1] * msg_in[n, 0 : GROUPS * ROWS].astype(f32)
    acc = (acc / total).reshape(GROUPS, REQ, PER, D)
    for g in range(GROUPS):
        tmp[pl.ds(g * ROWS, ROWS)] = acc[g].reshape(ROWS, D)
    for r in range(REQ):
        parts = [tmp[pl.ds(g * ROWS + r * PER, PER)] for g in range(GROUPS)]
        out_ref[r] = jnp.concatenate(parts, axis=0).astype(bf16)


def on_device(queries, prefix_keys, prefix_values, suffix_keys, suffix_values, suffix_lengths):
    anywhere = pl.BlockSpec(memory_space=pl.ANY)
    vmem = pl.BlockSpec(memory_space=pltpu.VMEM)
    dma = pltpu.SemaphoreType.DMA
    return pl.pallas_call(
        kernel,
        out_shape=jax.ShapeDtypeStruct(queries.shape, bf16),
        in_specs=[pl.BlockSpec(memory_space=pltpu.SMEM), vmem, anywhere, anywhere, anywhere, anywhere],
        out_specs=vmem,
        scratch_shapes=[
            pltpu.VMEM((GROUPS * KEYS, D), bf16),
            pltpu.VMEM((GROUPS * KEYS, D), bf16),
            pltpu.VMEM((REQ * SUF * GROUPS, D), bf16),
            pltpu.VMEM((REQ * SUF * GROUPS, D), bf16),
            pltpu.VMEM((1024, D), f32),
            pltpu.VMEM((GROUPS, KEYS, D), bf16),
            pltpu.VMEM((GROUPS, D, KEYS), bf16),
            pltpu.VMEM((GROUPS, X, 2, LANES, D), bf16),
            pltpu.VMEM((KEYS, LANES), f32),
            pltpu.VMEM((KEYS, LANES), f32),
            pltpu.VMEM((8, LANES), f32),
            pltpu.VMEM((8, LANES), f32),
            pltpu.VMEM((CHUNKS, GROUPS, 2, D + 16, HALF), f32),
            pltpu.VMEM((CHUNKS, GROUPS, D + 16, HALF), f32),
            pltpu.VMEM((2, GROUPS, D + 8, HALF), f32),
            pltpu.VMEM((X, 2, GROUPS, PART, HALF), bf16),
            pltpu.VMEM((X, 2, GROUPS, PART, HALF), bf16),
            pltpu.VMEM((Z, MSG, D), bf16),
            pltpu.VMEM((Z, MSG, D), bf16),
            pltpu.VMEM((GROUPS * ROWS, D), f32),
            pltpu.VMEM((GROUPS * ROWS, D), f32),
            dma((4,)),
            dma((Z,)), dma((Z,)),
            dma((X, 2)), dma((X, 2)),
            dma((X, 2)), dma((X, 2)),
            dma((CHUNKS, GROUPS)), dma((CHUNKS, GROUPS)),
            dma((X, 2, GROUPS)), dma((X, 2, GROUPS)),
            dma((Z,)), dma((Z,)),
        ],
        compiler_params=pltpu.CompilerParams(collective_id=0, has_side_effects=True, vmem_limit_bytes=56 * 2**20),
        cost_estimate=pl.CostEstimate(flops=9 * 10**9, bytes_accessed=9 * 2**20, transcendentals=17 * 10**6),
    )(
        suffix_lengths,
        queries,
        prefix_keys.reshape(GROUPS * KEYS, D),
        prefix_values.reshape(GROUPS * KEYS, D),
        suffix_keys.reshape(REQ * SUF * GROUPS, D),
        suffix_values.reshape(REQ * SUF * GROUPS, D),
    )


def solution(mesh):
    return jax.shard_map(
        on_device,
        mesh=mesh,
        in_specs=(
            P("pos", "kvh", None),
            P("pos", "kvh", None),
            P("pos", "kvh", None),
            P("pos", None, "kvh", None),
            P("pos", None, "kvh", None),
            P("pos"),
        ),
        out_specs=P("pos", "kvh", None),
        check_vma=False,
    )
```
